128 devices in a mesh: dp: 8 (over y, core), expert: 16 (over x, z).
Axes of the slice: x: 4, y: 4, z: 4, core: 2. Of those that a mesh axis runs over, the one named last changes fastest.
Arguments:
- tokens: bfloat16 [16384, 4096], P(('dp', 'expert')), may hold values from -6 to 6
- out_grad: bfloat16 [16384, 4096], P(('dp', 'expert')), may hold values from -6 to 6
- group_token: int32 [128, 16, 32], P(('dp', 'expert')), may hold values from 0 to 127, as said below
- group_count: int32 [128, 16], P(('dp', 'expert')), may hold values from 1 to 32, as said below
- group_prob: bfloat16 [128, 16, 32], P(('dp', 'expert')), may hold values from 0.049804688 to 1
- w_gate: bfloat16 [16, 4096, 768], P('expert'), may hold values from -0.09375 to 0.09375
- w_up: bfloat16 [16, 4096, 768], P('expert'), may hold values from -0.09375 to 0.09375
- w_down: bfloat16 [16, 768, 4096], P('expert'), may hold values from -0.21875 to 0.21875
Outputs:
- token_grad: bfloat16 [16384, 4096], P(('dp', 'expert'))
- route_grad: bfloat16 [128, 16, 32], P(('dp', 'expert'))
- grad_gate: bfloat16 [16, 4096, 768], P('expert', 'dp')
- grad_up: bfloat16 [16, 4096, 768], P('expert', 'dp')
- grad_down: bfloat16 [16, 768, 4096], P('expert', None, 'dp')
The draws below stay inside these ranges and needn't reach their ends.
Inputs may be any that keep to these rules, and one draw needn't show every extreme that they name: `group_token`: within one group (s, e) the 32 entries name distinct tokens of device s; entries of slots that are not live are arbitrary. `group_count`: in every draw some expert's group is full from every device, and every device has a full group.
All inputs are finite; a program needn't handle non-finite values.
Results may differ from the reference program's by a relative error of at most 0.018.
Values may be sent and summed in bfloat16 or wider, within the bound.
A program may use at most 128 MiB of HBM per device.

```python
import math
import jax
import jax.numpy as jnp
from jax import lax

D = 4096
FF = 768
TOK_DEV = 128
EXPERTS = 16
SOURCES = 128
CAP = 32
TOKENS = 16384
N_DP = 8


def draw_group_token(key, part):
    key = jax.random.fold_in(key, 11)
    scores = jax.random.randint(key, (SOURCES, EXPERTS, TOK_DEV), 0, 4096) * TOK_DEV
    scores = scores + jnp.arange(TOK_DEV, dtype=jnp.int32)
    order = jnp.argsort(scores, axis=-1, stable=True)
    return order[..., :CAP].astype(jnp.int32)


def draw_group_count(key, part):
    key = jax.random.fold_in(key, 23)
    first, second, third, fourth = jax.random.split(key, 4)
    upper = jax.random.randint(second, (EXPERTS,), CAP // 4, CAP + 1)
    counts = jax.random.randint(first, (SOURCES, EXPERTS), (upper // 2)[None, :], (upper + 1)[None, :])
    expert_ids = jnp.arange(EXPERTS, dtype=jnp.int32)
    hottest = jax.random.randint(third, (), 0, EXPERTS)
    counts = jnp.where(expert_ids[None, :] == hottest, CAP, counts)
    filled = jax.random.randint(fourth, (SOURCES, 1), 0, EXPERTS)
    counts = jnp.where(expert_ids[None, :] == filled, CAP, counts)
    return counts.astype(jnp.int32)


def block_levels(key, dims, pieces, smallest, largest):
    gain, own = 1.0, jax.random.fold_in(key, 6)
    for axis_at, parts in pieces:
        draws = jnp.exp(jax.random.uniform(jax.random.fold_in(own, axis_at), (parts,), jnp.float32, smallest / len(pieces), largest / len(pieces)))
        gain = gain * jnp.repeat(draws, dims[axis_at] // parts).reshape([-1 if axis == axis_at else 1 for axis in range(len(dims))])
    return gain


def gaussian(stream_key, extent, deviation, reach, shards=(), held_as=jnp.bfloat16):
    values = jax.random.normal(stream_key, extent, jnp.float32) * deviation
    if len(shards) > 0:
        values = block_levels(stream_key, extent, shards, -0.22, 0.18) * values
    return jnp.clip(values, min=-reach, max=reach).astype(held_as)


def setup_inputs(seed: int = 0) -> dict:
    streams_of = jax.random.split(jax.random.key(seed), 9)
    return {
        "tokens": gaussian(streams_of[0], (TOKENS, D), 1.0, 6.0, ((0, 128),)),
        "out_grad": gaussian(streams_of[1], (TOKENS, D), 1.0, 6.0, ((0, 128),)),
        "group_token": draw_group_token(jax.random.fold_in(streams_of[8], 71), 0),
        "group_count": draw_group_count(jax.random.fold_in(streams_of[8], 71), 0),
        "group_prob": jnp.clip(jnp.exp(math.log(1.0) - 2.9996462 * jax.random.uniform(streams_of[4], (SOURCES, EXPERTS, CAP), jnp.float32) ** block_levels(streams_of[4], (SOURCES, EXPERTS, CAP), ((0, 128),), -0.2, 0.2)), 0.049804688, 1.0).astype(jnp.bfloat16),
        "w_gate": gaussian(streams_of[5], (EXPERTS, D, FF), D ** -0.5, 0.09375, ((0, 16),)),
        "w_up": gaussian(streams_of[6], (EXPERTS, D, FF), D ** -0.5, 0.09375, ((0, 16),)),
        "w_down": gaussian(streams_of[7], (EXPERTS, FF, D), FF ** -0.5, 0.21875, ((0, 16),)),
    }


def settle(partial_sum):
    rounded = lax.optimization_barrier(partial_sum.astype(jnp.bfloat16))
    return (jnp.sum(rounded.astype(jnp.float32), axis=0) / N_DP).astype(jnp.bfloat16)


def reference(tokens, out_grad, group_token, group_count, group_prob, w_gate, w_up, w_down):
    by_source = tokens.reshape(SOURCES, TOK_DEV, D)
    grad_source = out_grad.reshape(SOURCES, TOK_DEV, D)
    slot_ids = jnp.arange(CAP, dtype=jnp.int32)
    source_ids = jnp.arange(SOURCES, dtype=jnp.int32)[:, None]
    zero_half = jnp.zeros((), jnp.bfloat16)

    def per_expert(token_acc, expert):
        index = group_token[:, expert, :].astype(jnp.int32)
        live_slot = slot_ids[None, :] < group_count[:, expert][:, None]
        slot_rows = jnp.where(live_slot[..., None], by_source[source_ids, index], zero_half).reshape(-1, D)
        slot_grads = jnp.where(live_slot[..., None], grad_source[source_ids, index], zero_half).reshape(-1, D)
        route_prob = jnp.where(live_slot, group_prob[:, expert, :], zero_half).reshape(-1)
        weight_gate = w_gate[expert]
        weight_up = w_up[expert]
        weight_down = w_down[expert]
        gate_pre = jnp.dot(slot_rows, weight_gate, preferred_element_type=jnp.float32)
        up_pre = jnp.dot(slot_rows, weight_up, preferred_element_type=jnp.float32)
        sigmoid_gate = jax.nn.sigmoid(gate_pre)
        activated = gate_pre * sigmoid_gate
        hidden = (activated * up_pre).astype(jnp.bfloat16)
        expert_out = jnp.dot(hidden, weight_down, preferred_element_type=jnp.float32).astype(jnp.bfloat16)
        prob_grad = jnp.sum(slot_grads.astype(jnp.float32) * expert_out.astype(jnp.float32), axis=-1).astype(jnp.bfloat16)
        output_grad = (route_prob.astype(jnp.float32)[:, None] * slot_grads.astype(jnp.float32)).astype(jnp.bfloat16)
        hidden_grad = jnp.dot(output_grad, weight_down.T, preferred_element_type=jnp.float32)
        gate_grad = (hidden_grad * up_pre * sigmoid_gate * (1.0 + gate_pre * (1.0 - sigmoid_gate))).astype(jnp.bfloat16)
        up_grad = (hidden_grad * activated).astype(jnp.bfloat16)
        input_grad = (jnp.dot(gate_grad, weight_gate.T, preferred_element_type=jnp.float32)
                      + jnp.dot(up_grad, weight_up.T, preferred_element_type=jnp.float32)).astype(jnp.bfloat16)
        token_acc = token_acc.at[source_ids, index].add(input_grad.reshape(SOURCES, CAP, D).astype(jnp.float32))
        grouped_rows = slot_rows.reshape(N_DP, -1, D).astype(jnp.float32)
        grouped_hidden = hidden.reshape(N_DP, -1, FF).astype(jnp.float32)
        part_gate = jnp.einsum("nrd,nrf->ndf", grouped_rows, gate_grad.reshape(N_DP, -1, FF).astype(jnp.float32))
        part_up = jnp.einsum("nrd,nrf->ndf", grouped_rows, up_grad.reshape(N_DP, -1, FF).astype(jnp.float32))
        part_down = jnp.einsum("nrf,nrd->nfd", grouped_hidden, output_grad.reshape(N_DP, -1, D).astype(jnp.float32))
        return token_acc, (settle(part_gate), settle(part_up), settle(part_down), prob_grad.reshape(SOURCES, CAP))

    start = jnp.zeros((SOURCES, TOK_DEV, D), jnp.float32)
    token_acc, stacked = lax.scan(per_expert, start, jnp.arange(EXPERTS, dtype=jnp.int32))
    grad_gate, grad_up, grad_down, prob_stack = stacked
    token_grad = token_acc.reshape(TOKENS, D).astype(jnp.bfloat16)
    route_grad = jnp.transpose(prob_stack, (1, 0, 2))
    return token_grad, route_grad, grad_gate, grad_up, grad_down
```

```python
import jax
import jax.numpy as jnp
from jax import lax
from jax.experimental import pallas as pl
from jax.experimental.pallas import tpu as pltpu
from jax.sharding import PartitionSpec as P

MESH = pl.DeviceIdType.MESH
BF = jnp.bfloat16
F32 = jnp.float32
D = 4096
FF = 768
TOK = 128
EXP = 16
CAP = 32
ROWS = EXP * CAP
NCH = 4
W = D // NCH
PIECE = W // 8
HALF = W // 2
UNITS = 3 * NCH
SEND = 3
NWGU = 2
NWD = 2


def feature(chunk, block):
    return (2 * (block % 4) + block // 4) * (D // 8) + chunk * PIECE


def contract(left, right, dims):
    return lax.dot_general(left, right, (dims, ((), ())), preferred_element_type=F32)


def body(
    pick_ref, pick_prob_ref, place_ref, prob_ref, tok_ref, dy_ref, wg_hbm, wu_hbm, wd_hbm,
    tg_ref, route_ref, gg_ref, gu_ref, gd_ref,
    send, got_x, got_y, wgu, wdn, acc, hgrad, hidden, grads, got_back, rbuf, got_r,
    lhs_t, own, mate_out, mate_in, total, far, near, relay,
    disp_s, disp_r, disp_l, back_s, back_r, back_l, rs_s, rs_r, rs_l, wgu_sem, wdn_sem,
    mate_s, mate_r, ring_s, ring_r,
):
    dp = lax.axis_index("dp")
    me = lax.axis_index("expert")
    y, core = dp // 2, lax.rem(dp, 2)
    x, z = me // 4, lax.rem(me, 4)

    def peer(k):
        return lax.rem(x + k // 4, 4) * 4 + lax.rem(z + lax.rem(k, 4), 4)

    def on_expert(e):
        return {"dp": dp, "expert": e}

    mate = {"dp": y * 2 + 1 - core, "expert": me}
    y_dn, y_up, y_far = lax.rem(y + 3, 4), lax.rem(y + 1, 4), lax.rem(y + 2, 4)
    side = ({"dp": y_dn * 2 + core, "expert": me}, {"dp": y_up * 2 + core, "expert": me})

    def each_peer(fn):
        def step(i, carry):
            fn(1 + i)
            return carry
        lax.fori_loop(0, EXP - 1, step, 0)

    def load_gu(chunk, slot):
        for b in range(8):
            rows = pl.ds(feature(chunk, b), PIECE)
            here = pl.ds(b * PIECE, PIECE)
            pltpu.make_async_copy(wg_hbm.at[rows, :], wgu.at[slot, here, pl.ds(0, FF)], wgu_sem.at[slot]).start()
            pltpu.make_async_copy(wu_hbm.at[rows, :], wgu.at[slot, here, pl.ds(FF, FF)], wgu_sem.at[slot]).start()

    def wait_gu(slot):
        pltpu.make_async_copy(wgu.at[slot], wgu.at[slot], wgu_sem.at[slot]).wait()

    def load_dn(chunk, slot):
        for b in range(8):
            pltpu.make_async_copy(
                wd_hbm.at[:, pl.ds(feature(chunk, b), PIECE)],
                wdn.at[slot, :, pl.ds(b * PIECE, PIECE)], wdn_sem.at[slot]).start()

    def wait_dn(slot):
        pltpu.make_async_copy(wdn.at[slot], wdn.at[slot], wdn_sem.at[slot]).wait()

    for c in range(NWGU):
        load_gu(c, c)
    for c in range(NWD):
        load_dn(c, c)

    barrier = pltpu.get_barrier_semaphore()

    def greet(k):
        pl.semaphore_signal(barrier, inc=1, device_id=on_expert(peer(k)), device_id_type=MESH)

    each_peer(greet)
    for there in (mate, side[0], side[1]):
        pl.semaphore_signal(barrier, inc=1, device_id=there, device_id_type=MESH)

    def gather(t):
        source, select = (tok_ref, pick_ref) if t < NCH else (dy_ref, pick_prob_ref)
        c = t % NCH
        for h in range(2):
            rhs = jnp.concatenate(
                [source[:, feature(c, 4 * h + b):feature(c, 4 * h + b) + PIECE] for b in range(4)], axis=1)
            rows = contract(select[...], rhs, ((1,), (0,))).astype(BF)
            send[t % SEND, :, :, h * HALF:(h + 1) * HALF] = rows.reshape(EXP, CAP, HALF)

    def landing(t):
        return (got_x if t < NCH else got_y).at[t % NCH]

    def disp_copy(t, k):
        return pltpu.make_async_remote_copy(
            src_ref=send.at[t % SEND, peer(k)], dst_ref=landing(t).at[me],
            send_sem=disp_s.at[t, k], recv_sem=disp_r.at[t, k],
            device_id=on_expert(peer(k)), device_id_type=MESH)

    def disp_local(t):
        return pltpu.make_async_copy(send.at[t % SEND, me], landing(t).at[me], disp_l.at[t])

    def disp_start(t):
        each_peer(lambda k: disp_copy(t, k).start())
        disp_local(t).start()

    def disp_sent(t):
        each_peer(lambda k: disp_copy(t, k).wait_send())

    def disp_wait(t):
        disp_local(t).wait()
        each_peer(lambda k: disp_copy(t, k).wait_recv())

    def unit(u):
        if u < NCH:
            return got_y.at[u], hidden, 0
        v = u - NCH
        return got_x.at[v // 2], grads, (v % 2) * FF

    def product(u, core_half, write):
        rows, right, col = unit(u)
        start = pl.multiple_of(core_half * HALF, HALF)
        lhs_t[...] = rows[:, :, pl.ds(start, HALF)].reshape(ROWS, HALF).T
        for n in range(3):
            cols = slice(n * 256, (n + 1) * 256)
            write(cols, contract(lhs_t[...], right[:, col + n * 256:col + (n + 1) * 256], ((1,), (0,))))

    def mate_copy(u):
        return pltpu.make_async_remote_copy(
            src_ref=mate_out.at[u % 2], dst_ref=mate_in.at[u], send_sem=mate_s.at[u], recv_sem=mate_r.at[u],
            device_id=mate, device_id_type=MESH)

    def ring_copy(u, i):
        kind, way = i // 2, i % 2
        lower, upper = pl.ds(0, PIECE // 2), pl.ds(PIECE // 2, PIECE // 2)
        owner = (y_far, (y_dn, y_up)[way], (y_dn, y_up)[way])[kind]
        part = (lower, upper)[(way, 1 - way, way)[kind]]
        return pltpu.make_async_remote_copy(
            src_ref=total.at[u % 3, owner, part, :], dst_ref=(far, near, relay)[kind].at[u, way],
            send_sem=ring_s.at[u, i], recv_sem=ring_r.at[u, i],
            device_id=side[way], device_id_type=MESH)

    def stage0(u):
        if u >= 2:
            mate_copy(u - 2).wait_send()

        def to_mate(cols, value):
            mate_out[u % 2, :, cols] = value.astype(BF)

        def to_own(cols, value):
            own[:, cols] = value

        product(u, 1 - core, to_mate)
        mate_copy(u).start()
        product(u, core, to_own)

    def stage1(u):
        if u >= 3:
            for i in range(6):
                ring_copy(u - 3, i).wait_send()
        mate_copy(u).wait_recv()
        for q in range(4):
            rows = slice(q * PIECE, (q + 1) * PIECE)
            total[u % 3, q] = (own[rows, :] + mate_in[u, rows, :].astype(F32)).astype(BF)
        for i in range(4):
            ring_copy(u, i).start()

    def stage2(u):
        half = PIECE // 2
        for way, owner in ((0, y_dn), (1, y_up)):
            ring_copy(u, way).wait_recv()
            rows = slice(way * half, (way + 1) * half)
            total[u % 3, owner, rows, :] = (
                total[u % 3, owner, rows, :].astype(F32) + far[u, way].astype(F32)).astype(BF)
            ring_copy(u, 4 + way).start()

    def stage3(u):
        half = PIECE // 2
        for i in range(2, 6):
            ring_copy(u, i).wait_recv()
        halves = []
        for h in range(2):
            rows = slice(h * half, (h + 1) * half)
            halves.append((total[u % 3, y, rows, :].astype(F32) + near[u, 1 - h].astype(F32)
                           + relay[u, h].astype(F32)) * 0.125)
        whole = jnp.concatenate(halves, axis=0)
        if u < NCH:
            gd_ref[:, u * PIECE:(u + 1) * PIECE] = whole.T.astype(BF)
        else:
            v = u - NCH
            (gg_ref, gu_ref)[v % 2][(v // 2) * PIECE:(v // 2 + 1) * PIECE, :] = whole.astype(BF)

    def tick(t):
        if 0 <= t - 1 < UNITS:
            stage1(t - 1)
        if t < UNITS:
            stage0(t)
        if 0 <= t - 2 < UNITS:
            stage2(t - 2)
        if 0 <= t - 3 < UNITS:
            stage3(t - 3)

    def forward(c):
        disp_wait(c)
        wait_gu(c % NWGU)

        def step(n, carry):
            cols = pl.ds(pl.multiple_of(n * 256, 256), 256)
            part = contract(got_x[c].reshape(ROWS, W), wgu[c % NWGU, :, cols], ((1,), (0,)))
            if c == 0:
                acc[:, cols] = part
            else:
                acc[:, cols] += part
            return carry

        lax.fori_loop(0, 2 * FF // 256, step, 0)
        load_gu((c + NWGU) % NCH, c % NWGU)

    def activate():
        def step(i, carry):
            rows = pl.ds(pl.multiple_of(i * CAP, CAP), CAP)
            gate, up = acc[rows, :FF], acc[rows, FF:]
            sig = jax.nn.sigmoid(gate)
            act = gate * sig
            hidden[rows, :] = (act * up).astype(BF)
            acc[rows, :FF] = up * sig * (1.0 + gate * (1.0 - sig))
            acc[rows, FF:] = act
            return carry

        lax.fori_loop(0, EXP, step, 0)

    def backward(c):
        disp_wait(NCH + c)
        wait_dn(c % NWD)
        rows = got_y[c].reshape(ROWS, W)
        for n in range(3):
            cols = slice(n * 256, (n + 1) * 256)
            part = contract(rows, wdn[c % NWD, cols, :], ((1,), (1,)))
            if c == 0:
                hgrad[:, cols] = part
            else:
                hgrad[:, cols] += part
        if c + NWD < NCH:
            load_dn(c + NWD, c % NWD)

    def route_copy(k):
        return pltpu.make_async_remote_copy(
            src_ref=rbuf.at[peer(k)], dst_ref=got_r.at[me], send_sem=rs_s.at[k], recv_sem=rs_r.at[k],
            device_id=on_expert(peer(k)), device_id_type=MESH)

    def route_local():
        return pltpu.make_async_copy(rbuf.at[me], got_r.at[me], rs_l.at[0])

    def differentiate():
        def step(i, carry):
            rows = pl.ds(pl.multiple_of(i * CAP, CAP), CAP)
            grad = hgrad[rows, :]
            grads[rows, :FF] = (grad * acc[rows, :FF]).astype(BF)
            grads[rows, FF:] = (grad * acc[rows, FF:]).astype(BF)
            dot = jnp.sum(grad * hidden[rows, :].astype(F32), axis=1, keepdims=True)
            rbuf[i] = jnp.broadcast_to(dot, (CAP, 128))
            return carry

        lax.fori_loop(0, EXP, step, 0)

    def back_copy(c, k):
        return pltpu.make_async_remote_copy(
            src_ref=got_y.at[c, peer(k)], dst_ref=got_back.at[c, me], send_sem=back_s.at[c, k],
            recv_sem=back_r.at[c, k], device_id=on_expert(peer(k)), device_id_type=MESH)

    def back_local(c):
        return pltpu.make_async_copy(got_y.at[c, me], got_back.at[c, me], back_l.at[c])

    def give_back(c):
        wait_gu(c % NWGU)
        for n in range(W // 256):
            cols = slice(n * 256, (n + 1) * 256)
            part = contract(grads[...], wgu[c % NWGU, cols, :], ((1,), (1,)))
            got_y[c, :, :, cols] = part.astype(BF).reshape(EXP, CAP, 256)
        each_peer(lambda k: back_copy(c, k).start())
        back_local(c).start()
        if c + NWGU < NCH:
            load_gu(c + NWGU, c % NWGU)

    def combine(c):
        back_local(c).wait()
        each_peer(lambda k: back_copy(c, k).wait_recv())
        for h in range(2):
            rows = got_back[c, :, :, h * HALF:(h + 1) * HALF].reshape(ROWS, HALF)
            part = contract(place_ref[...], rows, ((1,), (0,))).astype(BF)
            for b in range(4):
                f = feature(c, 4 * h + b)
                tg_ref[:, f:f + PIECE] = part[:, b * PIECE:(b + 1) * PIECE]

    gather(0)
    gather(1)
    pl.semaphore_wait(barrier, EXP - 1 + 3)
    disp_start(0)
    disp_start(1)
    gather(2)
    disp_start(2)
    for t in range(2 * NCH):
        if t < NCH:
            forward(t)
        if t == NCH - 1:
            activate()
        if t >= NCH:
            backward(t - NCH)
        if t + SEND < 2 * NCH:
            disp_sent(t)
            gather(t + SEND)
            disp_start(t + SEND)
        if t >= NCH:
            tick(t - NCH)
    differentiate()
    each_peer(lambda k: route_copy(k).start())
    route_local().start()
    last = UNITS + 3
    for t in range(NCH, last):
        tick(t)
        r = t - NCH
        if r < NCH:
            give_back(r)
        if r >= 3 and r % 2 == 1 and (r - 3) // 2 < NCH:
            combine((r - 3) // 2)
    route_local().wait()
    each_peer(lambda k: route_copy(k).wait_recv())
    lane = lax.broadcasted_iota(jnp.int32, (EXP, CAP, 128), 2)
    slot = lax.broadcasted_iota(jnp.int32, (EXP, CAP, 128), 1)
    dots = jnp.sum(jnp.where(lane == slot, got_r[...], 0.0), axis=1)[:, :CAP]
    prob = prob_ref[...].astype(F32)
    live = prob > 0.0
    route_ref[...] = jnp.where(live, dots / jnp.where(live, prob, 1.0), 0.0).astype(BF)
    for t in range(2 * NCH - SEND, 2 * NCH):
        disp_sent(t)
    for c in range(NCH):
        each_peer(lambda k: back_copy(c, k).wait_send())
    each_peer(lambda k: route_copy(k).wait_send())
    for u in range(UNITS - 2, UNITS):
        mate_copy(u).wait_send()
    for u in range(UNITS - 3, UNITS):
        for i in range(6):
            ring_copy(u, i).wait_send()


def shards(tokens, out_grad, group_token, group_count, group_prob, w_gate, w_up, w_down):
    index, prob = group_token[0], group_prob[0]
    live = lax.broadcasted_iota(jnp.int32, (EXP, CAP), 1) < group_count[0][:, None]
    index = jnp.where(live, index, -1).reshape(ROWS)
    prob = jnp.where(live, prob, jnp.zeros((), BF))
    hit = index[:, None] == lax.broadcasted_iota(jnp.int32, (ROWS, TOK), 1)
    pick = hit.astype(BF)
    pick_prob = jnp.where(hit, prob.reshape(ROWS)[:, None], jnp.zeros((), BF))
    place = (index[None, :] == lax.broadcasted_iota(jnp.int32, (TOK, ROWS), 0)).astype(BF)
    vmem = pl.BlockSpec(memory_space=pltpu.VMEM)
    hbm = pl.BlockSpec(memory_space=pl.ANY)
    dma = pltpu.SemaphoreType.DMA
    token_grad, route_grad, grad_gate, grad_up, grad_down = pl.pallas_call(
        body,
        out_shape=(
            jax.ShapeDtypeStruct((TOK, D), BF),
            jax.ShapeDtypeStruct((EXP, CAP), BF),
            jax.ShapeDtypeStruct((D // 8, FF), BF),
            jax.ShapeDtypeStruct((D // 8, FF), BF),
            jax.ShapeDtypeStruct((FF, D // 8), BF),
        ),
        in_specs=[vmem] * 6 + [hbm] * 3,
        out_specs=[vmem] * 5,
        scratch_shapes=[
            pltpu.VMEM((SEND, EXP, CAP, W), BF),
            pltpu.VMEM((NCH, EXP, CAP, W), BF),
            pltpu.VMEM((NCH, EXP, CAP, W), BF),
            pltpu.VMEM((NWGU, W, 2 * FF), BF),
            pltpu.VMEM((NWD, FF, W), BF),
            pltpu.VMEM((ROWS, 2 * FF), F32),
            pltpu.VMEM((ROWS, FF), F32),
            pltpu.VMEM((ROWS, FF), BF),
            pltpu.VMEM((ROWS, 2 * FF), BF),
            pltpu.VMEM((NCH, EXP, CAP, W), BF),
            pltpu.VMEM((EXP, CAP, 128), F32),
            pltpu.VMEM((EXP, CAP, 128), F32),
            pltpu.VMEM((HALF, ROWS), BF),
            pltpu.VMEM((HALF, FF), F32),
            pltpu.VMEM((2, HALF, FF), BF),
            pltpu.VMEM((UNITS, HALF, FF), BF),
            pltpu.VMEM((3, 4, PIECE, FF), BF),
            pltpu.VMEM((UNITS, 2, PIECE // 2, FF), BF),
            pltpu.VMEM((UNITS, 2, PIECE // 2, FF), BF),
            pltpu.VMEM((UNITS, 2, PIECE // 2, FF), BF),
            dma((2 * NCH, EXP)), dma((2 * NCH, EXP)), dma((2 * NCH,)),
            dma((NCH, EXP)), dma((NCH, EXP)), dma((NCH,)),
            dma((EXP,)), dma((EXP,)), dma((1,)),
            dma((NWGU,)), dma((NWD,)),
            dma((UNITS,)), dma((UNITS,)), dma((UNITS, 6)), dma((UNITS, 6)),
        ],
        compiler_params=pltpu.CompilerParams(
            collective_id=0, has_side_effects=True, vmem_limit_bytes=64 << 20),
        cost_estimate=pl.CostEstimate(flops=8 * 2 * ROWS * D * FF, bytes_accessed=40 << 20, transcendentals=ROWS * FF),
    )(pick, pick_prob, place, prob, tokens, out_grad, w_gate[0], w_up[0], w_down[0])
    return token_grad, route_grad[None], grad_gate[None], grad_up[None], grad_down[None]


def solution(mesh):
    slots = P(("dp", "expert"), None, None)
    rows = P(("dp", "expert"), None)
    experts = P("expert", None, None)
    return jax.shard_map(
        shards, mesh=mesh,
        in_specs=(rows, rows, slots, rows, slots, experts, experts, experts),
        out_specs=(rows, slots, P("expert", "dp", None), P("expert", "dp", None), P("expert", None, "dp")),
        check_vma=False)
```

```python
import jax
import jax.numpy as jnp
from jax import lax
from jax.experimental import pallas as pl
from jax.experimental.pallas import tpu as pltpu
from jax.sharding import PartitionSpec as P

MESH = pl.DeviceIdType.MESH
BF = jnp.bfloat16
F32 = jnp.float32
D = 4096
FF = 768
TOK = 128
EXP = 16
CAP = 32
ROWS = EXP * CAP
NCH = 4
W = D // NCH
PIECE = W // 8
HALF = W // 2
UNITS = 3 * NCH
SEND = 4
LINE = 4
STEPS = 4 * NCH
SLOTS = 8
OPEN, PASS, PICK = 7, 5, 2
NWGU = 2
NWD = 2


def feature(chunk, block):
    return (2 * (block % 4) + block // 4) * (D // 8) + chunk * PIECE


def contract(left, right, dims):
    return lax.dot_general(left, right, (dims, ((), ())), preferred_element_type=F32)


def body(
    index_ref, count_ref, prob_ref, tok_hbm, dy_hbm, wg_hbm, wu_hbm, wd_hbm,
    tg_hbm, route_ref, gg_hbm, gu_hbm, gd_hbm,
    pick_ref, place_ref, tg_ref, gg_ref, gu_ref, gd_ref, out_sem, weigh, line, send, got_x, got_y, wgu, wdn, acc, hgrad, hidden, grads, got_back, rbuf, got_r,
    lhs_t, own, mate_out, mate_in, total, far, near, relay,
    info_s, info_r, fill_sem, line_s, line_r, free, disp_s, disp_r, disp_l, back_s, back_r, back_l, rs_s, rs_r, rs_l, wgu_sem, wdn_sem,
    mate_s, mate_r, ring_s, ring_r,
):
    dp = lax.axis_index("dp")
    me = lax.axis_index("expert")
    y, core = dp // 2, lax.rem(dp, 2)
    x, z = me // 4, lax.rem(me, 4)

    def peer(k):
        return lax.rem(x + k // 4, 4) * 4 + lax.rem(z + lax.rem(k, 4), 4)

    def on_expert(e):
        return {"dp": dp, "expert": e}

    mate = {"dp": y * 2 + 1 - core, "expert": me}
    y_dn, y_up, y_far = lax.rem(y + 3, 4), lax.rem(y + 1, 4), lax.rem(y + 2, 4)
    side = ({"dp": y_dn * 2 + core, "expert": me}, {"dp": y_up * 2 + core, "expert": me})

    def each_peer(fn):
        def step(i, carry):
            fn(1 + i)
            return carry
        lax.fori_loop(0, EXP - 1, step, 0)

    def load_gu(chunk, slot):
        for b in range(8):
            rows = pl.ds(feature(chunk, b), PIECE)
            here = pl.ds(b * PIECE, PIECE)
            pltpu.make_async_copy(wg_hbm.at[rows, :], wgu.at[slot, here, pl.ds(0, FF)], wgu_sem.at[slot]).start()
            pltpu.make_async_copy(wu_hbm.at[rows, :], wgu.at[slot, here, pl.ds(FF, FF)], wgu_sem.at[slot]).start()

    def wait_gu(slot):
        pltpu.make_async_copy(wgu.at[slot], wgu.at[slot], wgu_sem.at[slot]).wait()

    def load_dn(chunk, slot):
        for b in range(8):
            pltpu.make_async_copy(
                wd_hbm.at[:, pl.ds(feature(chunk, b), PIECE)],
                wdn.at[slot, :, pl.ds(b * PIECE, PIECE)], wdn_sem.at[slot]).start()

    def wait_dn(slot):
        pltpu.make_async_copy(wdn.at[slot], wdn.at[slot], wdn_sem.at[slot]).wait()

    barrier = pltpu.get_barrier_semaphore()

    def greet(k):
        pl.semaphore_signal(barrier, inc=1, device_id=on_expert(peer(k)), device_id_type=MESH)

    each_peer(greet)
    for there in (mate, side[0], side[1]):
        pl.semaphore_signal(barrier, inc=1, device_id=there, device_id_type=MESH)

    def ends(t):
        return (x, lambda q: q * 4 + z) if t % 2 == 0 else (z, lambda q: x * 4 + q)

    def fill(t):
        source = tok_hbm if t < 2 * NCH else dy_hbm
        place = ends(t)[0]
        for b in range(4):
            pltpu.make_async_copy(
                source.at[:, pl.ds(feature((t // 2) % NCH, 4 * (t % 2) + b), PIECE)],
                line.at[t % SLOTS, place, :, pl.ds(b * PIECE, PIECE)], fill_sem.at[t]).start()

    def line_copy(t, i):
        place, expert_at = ends(t)
        up, dn = lax.rem(place + 1, LINE), lax.rem(place + 3, LINE)
        owner = (place, place, dn, up)[i]
        rows = (pl.ds(0, TOK), pl.ds(0, TOK), pl.ds(0, TOK // 2), pl.ds(TOK // 2, TOK // 2))[i]
        block = line.at[t % SLOTS, owner, rows, :]
        return pltpu.make_async_remote_copy(
            src_ref=block, dst_ref=block, send_sem=line_s.at[t, i], recv_sem=line_r.at[t, i],
            device_id=on_expert(expert_at((up, dn, up, dn)[i])), device_id_type=MESH)

    def open_line(t):
        place = ends(t)[0]
        whole = line.at[t % SLOTS, place]
        pltpu.make_async_copy(whole, whole, fill_sem.at[t]).wait()
        if t >= SLOTS:
            pl.semaphore_wait(free.at[t - SLOTS], 2)
        line_copy(t, 0).start()
        line_copy(t, 1).start()

    def pass_line(t):
        line_copy(t, 0).wait_recv()
        line_copy(t, 2).start()
        line_copy(t, 1).wait_recv()
        line_copy(t, 3).start()

    def info_copy(a, d):
        place, expert_at = ends(a)
        there = lax.rem(place + d, LINE)
        return pltpu.make_async_remote_copy(
            src_ref=weigh.at[there] if a == 0 else weigh.at[:, there], dst_ref=pick_ref.at[a, 1, place],
            send_sem=info_s.at[a, d], recv_sem=info_r.at[a, d],
            device_id=on_expert(expert_at(there)), device_id_type=MESH)

    def column(values):
        owner = lax.broadcasted_iota(jnp.int32, (ROWS, EXP), 0) // CAP
        spread = (owner == lax.broadcasted_iota(jnp.int32, (ROWS, EXP), 1)).astype(BF)
        table = contract(spread, values.astype(BF), ((1,), (0,)))
        slot = lax.rem(lax.broadcasted_iota(jnp.int32, (ROWS, CAP), 0), CAP)
        return jnp.sum(jnp.where(slot == lax.broadcasted_iota(jnp.int32, (ROWS, CAP), 1), table, 0.0),
                       axis=1, keepdims=True)

    def live_mask():
        own = lax.broadcasted_iota(jnp.int32, (EXP, EXP), 0) == lax.broadcasted_iota(jnp.int32, (EXP, EXP), 1)
        count = jnp.sum(jnp.where(own, jnp.broadcast_to(count_ref[...].astype(F32), (EXP, EXP)), 0.0),
                        axis=1, keepdims=True)
        return lax.broadcasted_iota(jnp.int32, (EXP, CAP), 1).astype(F32) < count

    def describe():
        token = column(jnp.where(live_mask(), index_ref[0].astype(F32), -1.0))
        prob = column(prob_ref[0])
        hit = token == lax.broadcasted_iota(jnp.int32, (ROWS, TOK), 1).astype(F32)
        rows = jnp.where(hit, jnp.broadcast_to(prob, (ROWS, TOK)), 0.0).astype(BF)
        weigh[...] = rows.reshape(LINE, LINE, CAP, TOK)

    def select(a):
        for d in range(1, LINE):
            info_copy(a, d).wait_recv()
        for q in range(LINE):
            pick_ref[a, 0, q] = jnp.where(pick_ref[a, 1, q].astype(F32) > 0.0, 1.0, 0.0).astype(BF)

    def selector():
        hit = weigh[...].reshape(ROWS, TOK).astype(F32) > 0.0
        place_ref[...] = jnp.where(hit, 1.0, 0.0).astype(BF).T

    def pick_rows(t):
        line_copy(t, 2).wait_recv()
        line_copy(t, 3).wait_recv()
        if t >= SEND:
            for d in range(1, LINE):
                disp_copy(t - SEND, d).wait_send()
        kind = 0 if t < 2 * NCH else 1
        for q in range(LINE):
            rows = contract(pick_ref[t % 2, kind, q].reshape(LINE * CAP, TOK), line[t % SLOTS, q], ((1,), (0,)))
            send[t % SEND, :, q] = rows.astype(BF).reshape(LINE, CAP, HALF)
        disp_local(t).start()
        for d in range(1, LINE):
            disp_copy(t, d).start()
        if t + SLOTS < STEPS:
            place, expert_at = ends(t)
            line_copy(t, 2).wait_send()
            line_copy(t, 3).wait_send()
            for q in (lax.rem(place + 1, LINE), lax.rem(place + 3, LINE)):
                pl.semaphore_signal(free.at[t], inc=1, device_id=on_expert(expert_at(q)), device_id_type=MESH)
            line_copy(t, 0).wait_send()
            line_copy(t, 1).wait_send()
            fill(t + SLOTS)

    def landing(t):
        buffer = (got_x if t < 2 * NCH else got_y).at[(t // 2) % NCH]
        cols = pl.ds((t % 2) * HALF, HALF)
        return buffer.at[:, z, :, cols] if t % 2 == 0 else buffer.at[x, :, :, cols]

    def disp_copy(t, d):
        place, expert_at = ends(t + 1)
        there = lax.rem(place + d, LINE)
        return pltpu.make_async_remote_copy(
            src_ref=send.at[t % SEND, there], dst_ref=landing(t),
            send_sem=disp_s.at[t, d], recv_sem=disp_r.at[t, d],
            device_id=on_expert(expert_at(there)), device_id_type=MESH)

    def disp_local(t):
        return pltpu.make_async_copy(send.at[t % SEND, ends(t + 1)[0]], landing(t), disp_l.at[t])

    def disp_wait(t):
        disp_local(t).wait()
        for d in range(1, LINE):
            disp_copy(t, d).wait_recv()

    def unit(u):
        if u < NCH:
            return got_y.at[u], hidden, 0
        v = u - NCH
        return got_x.at[v // 2], grads, (v % 2) * FF

    def product(u, core_half, write):
        rows, right, col = unit(u)
        start = pl.multiple_of(core_half * HALF, HALF)
        lhs_t[...] = rows[:, :, :, pl.ds(start, HALF)].reshape(ROWS, HALF).T
        for n in range(3):
            cols = slice(n * 256, (n + 1) * 256)
            write(cols, contract(lhs_t[...], right[:, col + n * 256:col + (n + 1) * 256], ((1,), (0,))))

    def mate_copy(u):
        return pltpu.make_async_remote_copy(
            src_ref=mate_out.at[u % 2], dst_ref=mate_in.at[u], send_sem=mate_s.at[u], recv_sem=mate_r.at[u],
            device_id=mate, device_id_type=MESH)

    def ring_copy(u, i):
        kind, way = i // 2, i % 2
        lower, upper = pl.ds(0, PIECE // 2), pl.ds(PIECE // 2, PIECE // 2)
        owner = (y_far, (y_dn, y_up)[way], (y_dn, y_up)[way])[kind]
        part = (lower, upper)[(way, 1 - way, way)[kind]]
        return pltpu.make_async_remote_copy(
            src_ref=total.at[u % 3, owner, part, :], dst_ref=(far, near, relay)[kind].at[u, way],
            send_sem=ring_s.at[u, i], recv_sem=ring_r.at[u, i],
            device_id=side[way], device_id_type=MESH)

    def stage0(u):
        if u >= 2:
            mate_copy(u - 2).wait_send()

        def to_mate(cols, value):
            mate_out[u % 2, :, cols] = value.astype(BF)

        def to_own(cols, value):
            own[:, cols] = value

        product(u, 1 - core, to_mate)
        mate_copy(u).start()
        product(u, core, to_own)

    def stage1(u):
        if u >= 3:
            for i in range(6):
                ring_copy(u - 3, i).wait_send()
        mate_copy(u).wait_recv()
        for q in range(4):
            rows = slice(q * PIECE, (q + 1) * PIECE)
            total[u % 3, q] = (own[rows, :] + mate_in[u, rows, :].astype(F32)).astype(BF)
        for i in range(4):
            ring_copy(u, i).start()

    def stage2(u):
        half = PIECE // 2
        for way, owner in ((0, y_dn), (1, y_up)):
            ring_copy(u, way).wait_recv()
            rows = slice(way * half, (way + 1) * half)
            total[u % 3, owner, rows, :] = (
                total[u % 3, owner, rows, :].astype(F32) + far[u, way].astype(F32)).astype(BF)
            ring_copy(u, 4 + way).start()

    def stage3(u):
        half = PIECE // 2
        for i in range(2, 6):
            ring_copy(u, i).wait_recv()
        halves = []
        for h in range(2):
            rows = slice(h * half, (h + 1) * half)
            halves.append((total[u % 3, y, rows, :].astype(F32) + near[u, 1 - h].astype(F32)
                           + relay[u, h].astype(F32)) * 0.125)
        whole = jnp.concatenate(halves, axis=0)
        if u < NCH:
            gd_ref[:, u * PIECE:(u + 1) * PIECE] = whole.T.astype(BF)
        else:
            v = u - NCH
            (gg_ref, gu_ref)[v % 2][(v // 2) * PIECE:(v // 2 + 1) * PIECE, :] = whole.astype(BF)

    def tick(t):
        if 0 <= t - 1 < UNITS:
            stage1(t - 1)
        if t < UNITS:
            stage0(t)
        if 0 <= t - 2 < UNITS:
            stage2(t - 2)
        if 0 <= t - 3 < UNITS:
            stage3(t - 3)

    def forward(c):
        disp_wait(2 * c)
        disp_wait(2 * c + 1)
        wait_gu(c % NWGU)

        def step(n, carry):
            cols = pl.ds(pl.multiple_of(n * 256, 256), 256)
            part = contract(got_x[c].reshape(ROWS, W), wgu[c % NWGU, :, cols], ((1,), (0,)))
            if c == 0:
                acc[:, cols] = part
            else:
                acc[:, cols] += part
            return carry

        lax.fori_loop(0, 2 * FF // 256, step, 0)
        load_gu((c + NWGU) % NCH, c % NWGU)

    def activate():
        def step(i, carry):
            rows = pl.ds(pl.multiple_of(i * CAP, CAP), CAP)
            gate, up = acc[rows, :FF], acc[rows, FF:]
            sig = jax.nn.sigmoid(gate)
            act = gate * sig
            hidden[rows, :] = (act * up).astype(BF)
            acc[rows, :FF] = up * sig * (1.0 + gate * (1.0 - sig))
            acc[rows, FF:] = act
            return carry

        lax.fori_loop(0, EXP, step, 0)

    def landed(c):
        disp_wait(2 * (NCH + c))
        disp_wait(2 * (NCH + c) + 1)

    def backward(c):
        if c < NCH - 1:
            landed(c)
        wait_dn(c % NWD)
        rows = got_y[c].reshape(ROWS, W)
        for n in range(3):
            cols = slice(n * 256, (n + 1) * 256)
            part = contract(rows, wdn[c % NWD, cols, :], ((1,), (1,)))
            if c == 0:
                hgrad[:, cols] = part
            else:
                hgrad[:, cols] += part
        if c + NWD < NCH:
            load_dn(c + NWD, c % NWD)

    def route_copy(k):
        return pltpu.make_async_remote_copy(
            src_ref=rbuf.at[peer(k)], dst_ref=got_r.at[me], send_sem=rs_s.at[k], recv_sem=rs_r.at[k],
            device_id=on_expert(peer(k)), device_id_type=MESH)

    def route_local():
        return pltpu.make_async_copy(rbuf.at[me], got_r.at[me], rs_l.at[0])

    def differentiate():
        def step(i, carry):
            rows = pl.ds(pl.multiple_of(i * CAP, CAP), CAP)
            grad = hgrad[rows, :]
            grads[rows, :FF] = (grad * acc[rows, :FF]).astype(BF)
            grads[rows, FF:] = (grad * acc[rows, FF:]).astype(BF)
            dot = jnp.sum(grad * hidden[rows, :].astype(F32), axis=1, keepdims=True)
            rbuf[i] = jnp.broadcast_to(dot, (CAP, 128))
            return carry

        lax.fori_loop(0, EXP, step, 0)

    def back_copy(c, k):
        return pltpu.make_async_remote_copy(
            src_ref=got_y.at[c, lax.rem(x + k // 4, 4), lax.rem(z + lax.rem(k, 4), 4)], dst_ref=got_back.at[c, me], send_sem=back_s.at[c, k],
            recv_sem=back_r.at[c, k], device_id=on_expert(peer(k)), device_id_type=MESH)

    def back_local(c):
        return pltpu.make_async_copy(got_y.at[c, x, z], got_back.at[c, me], back_l.at[c])

    def give_back(c):
        wait_gu(c % NWGU)
        for n in range(W // 256):
            cols = slice(n * 256, (n + 1) * 256)
            part = contract(grads[...], wgu[c % NWGU, cols, :], ((1,), (1,)))
            got_y[c, :, :, :, cols] = part.astype(BF).reshape(LINE, LINE, CAP, 256)
        each_peer(lambda k: back_copy(c, k).start())
        back_local(c).start()
        if c + NWGU < NCH:
            load_gu(c + NWGU, c % NWGU)

    def combine(c):
        back_local(c).wait()
        each_peer(lambda k: back_copy(c, k).wait_recv())
        for h in range(2):
            rows = got_back[c, :, :, h * HALF:(h + 1) * HALF].reshape(ROWS, HALF)
            part = contract(place_ref[...], rows, ((1,), (0,))).astype(BF)
            for b in range(4):
                f = feature(c, 4 * h + b)
                tg_ref[:, f:f + PIECE] = part[:, b * PIECE:(b + 1) * PIECE]

    def store(i, src, dst):
        return pltpu.make_async_copy(src, dst, out_sem.at[i])

    for t in range(SLOTS):
        fill(t)
    describe()
    pick_ref[0, 1, x] = weigh[x]
    pick_ref[1, 1, z] = weigh[:, z]
    pl.semaphore_wait(barrier, EXP - 1 + 3)
    open_line(0)
    open_line(1)
    for a in range(2):
        for d in range(1, LINE):
            info_copy(a, d).start()
    for t in range(2, 4):
        open_line(t)
    pass_line(0)
    pass_line(1)
    select(0)
    open_line(4)
    pick_rows(0)
    select(1)
    open_line(5)
    pick_rows(1)
    load_gu(0, 0)
    pass_line(2)
    open_line(6)
    pass_line(3)
    load_gu(1, 1)
    pass_line(4)
    for c in range(NWD):
        load_dn(c, c)
    for t in range(STEPS):
        if t + PASS < STEPS:
            pass_line(t + PASS)
        if t + OPEN < STEPS:
            open_line(t + OPEN)
        if t + PICK < STEPS:
            pick_rows(t + PICK)
        c = t // 2
        if t % 2 == 1:
            if c < NCH:
                forward(c)
            else:
                if t == STEPS - 1:
                    landed(NCH - 1)
                    stage0(NCH - 1)
                backward(c - NCH)
        if t == 2:
            selector()
        if t == 2 * NCH - 1:
            activate()
        u = c - NCH
        if 0 <= u < NCH - 1 and t % 2 == 1:
            stage0(u)
            if u >= 2:
                stage3(u - 2)
        if 1 <= u and t % 2 == 0:
            stage1(u - 1)
            if u >= 2:
                stage2(u - 2)
    differentiate()
    for t in range(NCH, UNITS + 3):
        stage1(t - 1) if t - 1 < UNITS else None
        stage0(t) if t < UNITS else None
        if NCH - 2 <= t - 2 < UNITS:
            stage2(t - 2)
        if t == NCH:
            stage3(NCH - 3)
        r = t - NCH
        if r < NCH:
            give_back(r)
        if r == NCH:
            each_peer(lambda k: route_copy(k).start())
            route_local().start()
        if NCH - 2 <= t - 3:
            stage3(t - 3)
        if r == 2:
            store(0, gd_ref, gd_hbm).start()
        if r >= 3 and r % 2 == 1 and (r - 3) // 2 < NCH:
            combine((r - 3) // 2)
        if t == UNITS + 1:
            store(1, gg_ref, gg_hbm).start()
            store(3, tg_ref, tg_hbm).start()
    store(2, gu_ref, gu_hbm).start()
    route_local().wait()
    each_peer(lambda k: route_copy(k).wait_recv())
    lane = lax.broadcasted_iota(jnp.int32, (EXP, CAP, 128), 2)
    slot = lax.broadcasted_iota(jnp.int32, (EXP, CAP, 128), 1)
    dots = jnp.sum(jnp.where(lane == slot, got_r[...], 0.0), axis=1)[:, :CAP]
    prob = prob_ref[0].astype(F32)
    live = live_mask()
    route_ref[0] = jnp.where(live, dots / jnp.where(live, prob, 1.0), 0.0).astype(BF)
    for a in range(2):
        for d in range(1, LINE):
            info_copy(a, d).wait_send()
    for t in range(STEPS - SLOTS, STEPS):
        for i in range(4):
            line_copy(t, i).wait_send()
    for t in range(STEPS - SEND, STEPS):
        for d in range(1, LINE):
            disp_copy(t, d).wait_send()
    for c in range(NCH):
        each_peer(lambda k: back_copy(c, k).wait_send())
    each_peer(lambda k: route_copy(k).wait_send())
    for u in range(UNITS - 2, UNITS):
        mate_copy(u).wait_send()
    for u in range(UNITS - 3, UNITS):
        for i in range(6):
            ring_copy(u, i).wait_send()
    for i, (src, dst) in enumerate(((gd_ref, gd_hbm), (gg_ref, gg_hbm), (gu_ref, gu_hbm), (tg_ref, tg_hbm))):
        store(i, src, dst).wait()


def finish(*refs):
    sources, results, held, sems = refs[:5], refs[5:10], refs[10:15], refs[15]
    loads = [pltpu.make_async_copy(a, b, sems.at[0, i]) for i, (a, b) in enumerate(zip(sources, held))]
    stores = [pltpu.make_async_copy(a, b, sems.at[1, i]) for i, (a, b) in enumerate(zip(held, results))]
    for copy in loads:
        copy.start()
    for i in (1, 2, 3, 4, 0):
        loads[i].wait()
        stores[i].start()
    for copy in stores:
        copy.wait()


def shards(tokens, out_grad, group_token, group_count, group_prob, w_gate, w_up, w_down):
    vmem = pl.BlockSpec(memory_space=pltpu.VMEM)
    hbm = pl.BlockSpec(memory_space=pl.ANY)
    dma = pltpu.SemaphoreType.DMA
    results = pl.pallas_call(
        body,
        out_shape=(
            jax.ShapeDtypeStruct((TOK, D), BF),
            jax.ShapeDtypeStruct((1, EXP, CAP), BF),
            jax.ShapeDtypeStruct((D // 8, FF), BF),
            jax.ShapeDtypeStruct((D // 8, FF), BF),
            jax.ShapeDtypeStruct((FF, D // 8), BF),
        ),
        in_specs=[vmem] * 3 + [hbm] * 5,
        out_specs=[hbm, vmem, hbm, hbm, hbm],
        scratch_shapes=[
            pltpu.VMEM((2, 2, LINE, LINE, CAP, TOK), BF),
            pltpu.VMEM((TOK, ROWS), BF),
            pltpu.VMEM((TOK, D), BF),
            pltpu.VMEM((D // 8, FF), BF), pltpu.VMEM((D // 8, FF), BF), pltpu.VMEM((FF, D // 8), BF),
            dma((4,)),
            pltpu.VMEM((LINE, LINE, CAP, TOK), BF),
            pltpu.VMEM((SLOTS, LINE, TOK, HALF), BF),
            pltpu.VMEM((SEND, LINE, LINE, CAP, HALF), BF),
            pltpu.VMEM((NCH, LINE, LINE, CAP, W), BF),
            pltpu.VMEM((NCH, LINE, LINE, CAP, W), BF),
            pltpu.VMEM((NWGU, W, 2 * FF), BF),
            pltpu.VMEM((NWD, FF, W), BF),
            pltpu.VMEM((ROWS, 2 * FF), F32),
            pltpu.VMEM((ROWS, FF), F32),
            pltpu.VMEM((ROWS, FF), BF),
            pltpu.VMEM((ROWS, 2 * FF), BF),
            pltpu.VMEM((NCH, EXP, CAP, W), BF),
            pltpu.VMEM((EXP, CAP, 128), F32),
            pltpu.VMEM((EXP, CAP, 128), F32),
            pltpu.VMEM((HALF, ROWS), BF),
            pltpu.VMEM((HALF, FF), F32),
            pltpu.VMEM((2, HALF, FF), BF),
            pltpu.VMEM((UNITS, HALF, FF), BF),
            pltpu.VMEM((3, 4, PIECE, FF), BF),
            pltpu.VMEM((UNITS, 2, PIECE // 2, FF), BF),
            pltpu.VMEM((UNITS, 2, PIECE // 2, FF), BF),
            pltpu.VMEM((UNITS, 2, PIECE // 2, FF), BF),
            dma((2, LINE)), dma((2, LINE)), dma((STEPS,)), dma((STEPS, 4)), dma((STEPS, 4)),
            pltpu.SemaphoreType.REGULAR((SLOTS,)),
            dma((STEPS, LINE)), dma((STEPS, LINE)), dma((STEPS,)),
            dma((NCH, EXP)), dma((NCH, EXP)), dma((NCH,)),
            dma((EXP,)), dma((EXP,)), dma((1,)),
            dma((NWGU,)), dma((NWD,)),
            dma((UNITS,)), dma((UNITS,)), dma((UNITS, 6)), dma((UNITS, 6)),
        ],
        compiler_params=pltpu.CompilerParams(
            collective_id=0, has_side_effects=True, vmem_limit_bytes=64 << 20),
        cost_estimate=pl.CostEstimate(flops=8 * 2 * ROWS * D * FF, bytes_accessed=40 << 20, transcendentals=ROWS * FF),
    )(group_token, group_count, group_prob, tokens, out_grad, w_gate[0], w_up[0], w_down[0])
    token_grad, route_grad, grad_gate, grad_up, grad_down = pl.pallas_call(
        finish,
        out_shape=tuple(jax.ShapeDtypeStruct(r.shape, r.dtype) for r in results),
        in_specs=[hbm] * 5,
        out_specs=[hbm] * 5,
        scratch_shapes=[pltpu.VMEM(r.shape, r.dtype) for r in results] + [dma((2, 5))],
        compiler_params=pltpu.CompilerParams(vmem_limit_bytes=60 << 20),
    )(*results)
    return token_grad, route_grad, grad_gate[None], grad_up[None], grad_down[None]


def solution(mesh):
    slots = P(("dp", "expert"), None, None)
    rows = P(("dp", "expert"), None)
    experts = P("expert", None, None)
    return jax.shard_map(
        shards, mesh=mesh,
        in_specs=(rows, rows, slots, rows, slots, experts, experts, experts),
        out_specs=(rows, slots, P("expert", "dp", None), P("expert", "dp", None), P("expert", None, "dp")),
        check_vma=False)
```

```python
import jax
import jax.numpy as jnp
from jax import lax
from jax.experimental import pallas as pl
from jax.experimental.pallas import tpu as pltpu
from jax.sharding import PartitionSpec as P

MESH = pl.DeviceIdType.MESH
BF = jnp.bfloat16
F32 = jnp.float32
D = 4096
FF = 768
TOK = 128
EXP = 16
CAP = 32
ROWS = EXP * CAP
NCH = 4
W = D // NCH
PIECE = W // 8
HALF = W // 2
UNITS = 3 * NCH
SEND = 4
LINE = 4
STEPS = 4 * NCH
SLOTS = 8
OPEN, PASS, PICK = 7, 5, 2
NWGU = 2
NWD = 2


def feature(chunk, block):
    return (2 * (block % 4) + block // 4) * (D // 8) + chunk * PIECE


def contract(left, right, dims):
    return lax.dot_general(left, right, (dims, ((), ())), preferred_element_type=F32)


def body(
    index_hbm, count_hbm, prob_hbm, tok_hbm, dy_hbm, wg_hbm, wu_hbm, wd_hbm,
    tg_hbm, route_hbm, gg_hbm, gu_hbm, gd_hbm,
    index_ref, count_ref, prob_ref, route_ref, in_sem, pick_ref, place_ref, tg_ref, gg_ref, gu_ref, gd_ref, out_sem, weigh, line, send, got_x, got_y, wgu, wdn, acc, hgrad, hidden, grads, got_back, rbuf, got_r,
    lhs_t, own, mate_out, mate_in, total, far, near, relay,
    info_s, info_r, fill_sem, line_s, line_r, free, disp_s, disp_r, back_s, back_r, rs_s, rs_r, wgu_sem, wdn_sem,
    mate_s, mate_r, ring_s, ring_r,
):
    dp = lax.axis_index("dp")
    me = lax.axis_index("expert")
    y, core = dp // 2, lax.rem(dp, 2)
    x, z = me // 4, lax.rem(me, 4)

    def peer(k):
        return lax.rem(x + k // 4, 4) * 4 + lax.rem(z + lax.rem(k, 4), 4)

    def on_expert(e):
        return {"dp": dp, "expert": e}

    mate = {"dp": y * 2 + 1 - core, "expert": me}
    y_dn, y_up, y_far = lax.rem(y + 3, 4), lax.rem(y + 1, 4), lax.rem(y + 2, 4)
    side = ({"dp": y_dn * 2 + core, "expert": me}, {"dp": y_up * 2 + core, "expert": me})

    def each_peer(fn):
        def step(i, carry):
            fn(1 + i)
            return carry
        lax.fori_loop(0, EXP - 1, step, 0)

    def wait_bytes(like, sem):
        pltpu.make_async_copy(like, like, sem).wait()

    def load_gu(chunk, slot):
        for b in range(8):
            rows = pl.ds(feature(chunk, b), PIECE)
            here = pl.ds(b * PIECE, PIECE)
            pltpu.make_async_copy(wg_hbm.at[rows, :], wgu.at[slot, here, pl.ds(0, FF)], wgu_sem.at[slot]).start()
            pltpu.make_async_copy(wu_hbm.at[rows, :], wgu.at[slot, here, pl.ds(FF, FF)], wgu_sem.at[slot]).start()

    def wait_gu(slot):
        pltpu.make_async_copy(wgu.at[slot], wgu.at[slot], wgu_sem.at[slot]).wait()

    def load_dn(chunk, slot):
        for b in range(8):
            pltpu.make_async_copy(
                wd_hbm.at[:, pl.ds(feature(chunk, b), PIECE)],
                wdn.at[slot, :, pl.ds(b * PIECE, PIECE)], wdn_sem.at[slot]).start()

    def wait_dn(slot):
        pltpu.make_async_copy(wdn.at[slot], wdn.at[slot], wdn_sem.at[slot]).wait()

    barrier = pltpu.get_barrier_semaphore()

    def greet(k):
        pl.semaphore_signal(barrier, inc=1, device_id=on_expert(peer(k)), device_id_type=MESH)

    each_peer(greet)
    for there in (mate, side[0], side[1]):
        pl.semaphore_signal(barrier, inc=1, device_id=there, device_id_type=MESH)

    def ends(t):
        return (x, lambda q: q * 4 + z) if t % 2 == 0 else (z, lambda q: x * 4 + q)

    def fill(t):
        source = tok_hbm if t < 2 * NCH else dy_hbm
        place = ends(t)[0]
        for b in range(4):
            pltpu.make_async_copy(
                source.at[:, pl.ds(feature((t // 2) % NCH, 4 * (t % 2) + b), PIECE)],
                line.at[t % SLOTS, place, :, pl.ds(b * PIECE, PIECE)], fill_sem.at[t % SLOTS]).start()

    def line_copy(t, i):
        place, expert_at = ends(t)
        up, dn = lax.rem(place + 1, LINE), lax.rem(place + 3, LINE)
        owner = (place, place, dn, up)[i]
        rows = (pl.ds(0, TOK), pl.ds(0, TOK), pl.ds(0, TOK // 2), pl.ds(TOK // 2, TOK // 2))[i]
        block = line.at[t % SLOTS, owner, rows, :]
        return pltpu.make_async_remote_copy(
            src_ref=block, dst_ref=block, send_sem=line_s.at[t % SLOTS], recv_sem=line_r.at[t % SLOTS, min(i, 2)],
            device_id=on_expert(expert_at((up, dn, up, dn)[i])), device_id_type=MESH)

    def line_sent(t):
        wait_bytes(line.at[t % SLOTS, pl.ds(0, 3)], line_s.at[t % SLOTS])

    def open_line(t):
        place = ends(t)[0]
        whole = line.at[t % SLOTS, place]
        pltpu.make_async_copy(whole, whole, fill_sem.at[t % SLOTS]).wait()
        if t >= SLOTS:
            pl.semaphore_wait(free.at[t - SLOTS], 2)
        line_copy(t, 0).start()
        line_copy(t, 1).start()

    def pass_line(t):
        line_copy(t, 0).wait_recv()
        line_copy(t, 2).start()
        line_copy(t, 1).wait_recv()
        line_copy(t, 3).start()

    def info_copy(a, d):
        place, expert_at = ends(a)
        there = lax.rem(place + d, LINE)
        return pltpu.make_async_remote_copy(
            src_ref=weigh.at[there] if a == 0 else weigh.at[:, there], dst_ref=pick_ref.at[a, 1, place],
            send_sem=info_s.at[a], recv_sem=info_r.at[a],
            device_id=on_expert(expert_at(there)), device_id_type=MESH)

    def column(values):
        owner = lax.broadcasted_iota(jnp.int32, (ROWS, EXP), 0) // CAP
        spread = (owner == lax.broadcasted_iota(jnp.int32, (ROWS, EXP), 1)).astype(BF)
        table = contract(spread, values.astype(BF), ((1,), (0,)))
        slot = lax.rem(lax.broadcasted_iota(jnp.int32, (ROWS, CAP), 0), CAP)
        return jnp.sum(jnp.where(slot == lax.broadcasted_iota(jnp.int32, (ROWS, CAP), 1), table, 0.0),
                       axis=1, keepdims=True)

    def live_mask():
        own = lax.broadcasted_iota(jnp.int32, (EXP, EXP), 0) == lax.broadcasted_iota(jnp.int32, (EXP, EXP), 1)
        count = jnp.sum(jnp.where(own, jnp.broadcast_to(count_ref[...].astype(F32), (EXP, EXP)), 0.0),
                        axis=1, keepdims=True)
        return lax.broadcasted_iota(jnp.int32, (EXP, CAP), 1).astype(F32) < count

    def describe():
        token = column(jnp.where(live_mask(), index_ref[0].astype(F32), -1.0))
        prob = column(prob_ref[0])
        hit = token == lax.broadcasted_iota(jnp.int32, (ROWS, TOK), 1).astype(F32)
        rows = jnp.where(hit, jnp.broadcast_to(prob, (ROWS, TOK)), 0.0).astype(BF)
        weigh[...] = rows.reshape(LINE, LINE, CAP, TOK)

    def select(a):
        wait_bytes(weigh.at[pl.ds(0, 3)], info_r.at[a])
        for q in range(LINE):
            pick_ref[a, 0, q] = jnp.where(pick_ref[a, 1, q].astype(F32) > 0.0, 1.0, 0.0).astype(BF)

    def selector():
        hit = weigh[...].reshape(ROWS, TOK).astype(F32) > 0.0
        place_ref[...] = jnp.where(hit, 1.0, 0.0).astype(BF).T

    def pick_rows(t):
        wait_bytes(line.at[t % SLOTS, 0], line_r.at[t % SLOTS, 2])
        if t >= SEND:
            disp_sent(t - SEND)
        kind = 0 if t < 2 * NCH else 1
        for q in range(LINE):
            rows = contract(pick_ref[t % 2, kind, q].reshape(LINE * CAP, TOK), line[t % SLOTS, q], ((1,), (0,)))
            send[t % SEND, :, q] = rows.astype(BF).reshape(LINE, CAP, HALF)
        disp_local(t).start()
        for d in range(1, LINE):
            disp_copy(t, d).start()
        if t + SLOTS < STEPS:
            place, expert_at = ends(t)
            line_sent(t)
            for q in (lax.rem(place + 1, LINE), lax.rem(place + 3, LINE)):
                pl.semaphore_signal(free.at[t], inc=1, device_id=on_expert(expert_at(q)), device_id_type=MESH)
            fill(t + SLOTS)

    def landing(t):
        buffer = (got_x if t < 2 * NCH else got_y).at[(t // 2) % NCH]
        cols = pl.ds((t % 2) * HALF, HALF)
        return buffer.at[:, z, :, cols] if t % 2 == 0 else buffer.at[x, :, :, cols]

    def disp_copy(t, d):
        place, expert_at = ends(t + 1)
        there = lax.rem(place + d, LINE)
        return pltpu.make_async_remote_copy(
            src_ref=send.at[t % SEND, there], dst_ref=landing(t),
            send_sem=disp_s.at[t % SEND], recv_sem=disp_r.at[t],
            device_id=on_expert(expert_at(there)), device_id_type=MESH)

    def disp_local(t):
        return pltpu.make_async_copy(send.at[t % SEND, ends(t + 1)[0]], landing(t), disp_r.at[t])

    def disp_sent(t):
        wait_bytes(send.at[t % SEND, pl.ds(0, 3)], disp_s.at[t % SEND])

    def disp_wait(t):
        buffer = (got_x if t < 2 * NCH else got_y).at[(t // 2) % NCH]
        wait_bytes(buffer.at[:, :, :, pl.ds((t % 2) * HALF, HALF)], disp_r.at[t])

    def unit(u):
        if u < NCH:
            return got_y.at[u], hidden, 0
        v = u - NCH
        return got_x.at[v // 2], grads, (v % 2) * FF

    def product(u, core_half, write):
        rows, right, col = unit(u)
        start = pl.multiple_of(core_half * HALF, HALF)
        lhs_t[...] = rows[:, :, :, pl.ds(start, HALF)].reshape(ROWS, HALF).T
        for n in range(3):
            cols = slice(n * 256, (n + 1) * 256)
            write(cols, contract(lhs_t[...], right[:, col + n * 256:col + (n + 1) * 256], ((1,), (0,))))

    def mate_copy(u):
        return pltpu.make_async_remote_copy(
            src_ref=mate_out.at[u % 2], dst_ref=mate_in.at[u], send_sem=mate_s.at[u % 2], recv_sem=mate_r.at[u],
            device_id=mate, device_id_type=MESH)

    def ring_copy(u, i):
        kind, way = i // 2, i % 2
        lower, upper = pl.ds(0, PIECE // 2), pl.ds(PIECE // 2, PIECE // 2)
        owner = (y_far, (y_dn, y_up)[way], (y_dn, y_up)[way])[kind]
        part = (lower, upper)[(way, 1 - way, way)[kind]]
        return pltpu.make_async_remote_copy(
            src_ref=total.at[u % 3, owner, part, :], dst_ref=(far, near, relay)[kind].at[u, way],
            send_sem=ring_s.at[u % 3], recv_sem=ring_r.at[u, min(i, 2)],
            device_id=side[way], device_id_type=MESH)

    def ring_sent(u):
        wait_bytes(total.at[u % 3, pl.ds(0, 3)], ring_s.at[u % 3])

    def stage0(u):
        if u >= 2:
            mate_copy(u - 2).wait_send()

        def to_mate(cols, value):
            mate_out[u % 2, :, cols] = value.astype(BF)

        def to_own(cols, value):
            own[:, cols] = value

        product(u, 1 - core, to_mate)
        mate_copy(u).start()
        product(u, core, to_own)

    def stage1(u):
        if u >= 3:
            ring_sent(u - 3)
        mate_copy(u).wait_recv()
        for q in range(4):
            rows = slice(q * PIECE, (q + 1) * PIECE)
            total[u % 3, q] = (own[rows, :] + mate_in[u, rows, :].astype(F32)).astype(BF)
        for i in range(4):
            ring_copy(u, i).start()

    def stage2(u):
        half = PIECE // 2
        for way, owner in ((0, y_dn), (1, y_up)):
            ring_copy(u, way).wait_recv()
            rows = slice(way * half, (way + 1) * half)
            total[u % 3, owner, rows, :] = (
                total[u % 3, owner, rows, :].astype(F32) + far[u, way].astype(F32)).astype(BF)
            ring_copy(u, 4 + way).start()

    def stage3(u):
        half = PIECE // 2
        wait_bytes(total.at[0, pl.ds(0, 2)], ring_r.at[u, 2])
        halves = []
        for h in range(2):
            rows = slice(h * half, (h + 1) * half)
            halves.append((total[u % 3, y, rows, :].astype(F32) + near[u, 1 - h].astype(F32)
                           + relay[u, h].astype(F32)) * 0.125)
        whole = jnp.concatenate(halves, axis=0)
        if u < NCH:
            gd_ref[:, u * PIECE:(u + 1) * PIECE] = whole.T.astype(BF)
        else:
            v = u - NCH
            (gg_ref, gu_ref)[v % 2][(v // 2) * PIECE:(v // 2 + 1) * PIECE, :] = whole.astype(BF)

    def tick(t):
        if 0 <= t - 1 < UNITS:
            stage1(t - 1)
        if t < UNITS:
            stage0(t)
        if 0 <= t - 2 < UNITS:
            stage2(t - 2)
        if 0 <= t - 3 < UNITS:
            stage3(t - 3)

    def forward(c):
        disp_wait(2 * c)
        disp_wait(2 * c + 1)
        wait_gu(c % NWGU)

        def step(n, carry):
            cols = pl.ds(pl.multiple_of(n * 256, 256), 256)
            part = contract(got_x[c].reshape(ROWS, W), wgu[c % NWGU, :, cols], ((1,), (0,)))
            if c == 0:
                acc[:, cols] = part
            else:
                acc[:, cols] += part
            return carry

        lax.fori_loop(0, 2 * FF // 256, step, 0)
        load_gu((c + NWGU) % NCH, c % NWGU)

    def activate():
        def step(i, carry):
            rows = pl.ds(pl.multiple_of(i * CAP, CAP), CAP)
            gate, up = acc[rows, :FF], acc[rows, FF:]
            sig = jax.nn.sigmoid(gate)
            act = gate * sig
            hidden[rows, :] = (act * up).astype(BF)
            acc[rows, :FF] = up * sig * (1.0 + gate * (1.0 - sig))
            acc[rows, FF:] = act
            return carry

        lax.fori_loop(0, EXP, step, 0)

    def landed(c):
        disp_wait(2 * (NCH + c))
        disp_wait(2 * (NCH + c) + 1)

    def backward(c):
        if c < NCH - 1:
            landed(c)
        wait_dn(c % NWD)
        rows = got_y[c].reshape(ROWS, W)
        for n in range(3):
            cols = slice(n * 256, (n + 1) * 256)
            part = contract(rows, wdn[c % NWD, cols, :], ((1,), (1,)))
            if c == 0:
                hgrad[:, cols] = part
            else:
                hgrad[:, cols] += part
        if c + NWD < NCH:
            load_dn(c + NWD, c % NWD)

    def route_copy(k):
        return pltpu.make_async_remote_copy(
            src_ref=rbuf.at[peer(k)], dst_ref=got_r.at[me], send_sem=rs_s.at[0], recv_sem=rs_r.at[0],
            device_id=on_expert(peer(k)), device_id_type=MESH)

    def route_local():
        return pltpu.make_async_copy(rbuf.at[me], got_r.at[me], rs_r.at[0])

    def differentiate():
        def step(i, carry):
            rows = pl.ds(pl.multiple_of(i * CAP, CAP), CAP)
            grad = hgrad[rows, :]
            grads[rows, :FF] = (grad * acc[rows, :FF]).astype(BF)
            grads[rows, FF:] = (grad * acc[rows, FF:]).astype(BF)
            dot = jnp.sum(grad * hidden[rows, :].astype(F32), axis=1, keepdims=True)
            rbuf[i] = jnp.broadcast_to(dot, (CAP, 128))
            return carry

        lax.fori_loop(0, EXP, step, 0)

    def back_copy(c, k):
        return pltpu.make_async_remote_copy(
            src_ref=got_y.at[c, lax.rem(x + k // 4, 4), lax.rem(z + lax.rem(k, 4), 4)], dst_ref=got_back.at[c, me], send_sem=back_s.at[c],
            recv_sem=back_r.at[c], device_id=on_expert(peer(k)), device_id_type=MESH)

    def back_local(c):
        return pltpu.make_async_copy(got_y.at[c, x, z], got_back.at[c, me], back_r.at[c])

    def give_back(c):
        wait_gu(c % NWGU)
        for n in range(W // 256):
            cols = slice(n * 256, (n + 1) * 256)
            part = contract(grads[...], wgu[c % NWGU, cols, :], ((1,), (1,)))
            got_y[c, :, :, :, cols] = part.astype(BF).reshape(LINE, LINE, CAP, 256)
        each_peer(lambda k: back_copy(c, k).start())
        back_local(c).start()
        if c + NWGU < NCH:
            load_gu(c + NWGU, c % NWGU)

    def combine(c):
        wait_bytes(got_back.at[c], back_r.at[c])
        for h in range(2):
            rows = got_back[c, :, :, h * HALF:(h + 1) * HALF].reshape(ROWS, HALF)
            part = contract(place_ref[...], rows, ((1,), (0,))).astype(BF)
            for b in range(4):
                f = feature(c, 4 * h + b)
                tg_ref[:, f:f + PIECE] = part[:, b * PIECE:(b + 1) * PIECE]

    def store(i, src, dst):
        return pltpu.make_async_copy(src, dst, out_sem.at[i])

    small = [pltpu.make_async_copy(a, b, in_sem.at[i]) for i, (a, b) in enumerate(
        ((index_hbm, index_ref), (count_hbm, count_ref), (prob_hbm, prob_ref)))]
    for copy in small:
        copy.start()
    for t in range(SLOTS):
        fill(t)
    for copy in small:
        copy.wait()
    describe()
    pick_ref[0, 1, x] = weigh[x]
    pick_ref[1, 1, z] = weigh[:, z]
    pl.semaphore_wait(barrier, EXP - 1 + 3)
    open_line(0)
    open_line(1)
    for a in range(2):
        for d in range(1, LINE):
            info_copy(a, d).start()
    for t in range(2, 4):
        open_line(t)
    pass_line(0)
    pass_line(1)
    select(0)
    open_line(4)
    pick_rows(0)
    select(1)
    open_line(5)
    pick_rows(1)
    load_gu(0, 0)
    pass_line(2)
    open_line(6)
    pass_line(3)
    load_gu(1, 1)
    pass_line(4)
    for c in range(NWD):
        load_dn(c, c)
    for t in range(STEPS):
        if t + PASS < STEPS:
            pass_line(t + PASS)
        if t + OPEN < STEPS:
            open_line(t + OPEN)
        if t + PICK < STEPS:
            pick_rows(t + PICK)
        c = t // 2
        if t % 2 == 1:
            if c < NCH:
                forward(c)
            else:
                if t == STEPS - 1:
                    landed(NCH - 1)
                    stage0(NCH - 1)
                backward(c - NCH)
        if t == 2:
            selector()
        if t == 2 * NCH - 1:
            activate()
        u = c - NCH
        if 0 <= u < NCH - 1 and t % 2 == 1:
            stage0(u)
            if u >= 2:
                stage3(u - 2)
        if 1 <= u and t % 2 == 0:
            stage1(u - 1)
            if u >= 2:
                stage2(u - 2)
    differentiate()
    for t in range(NCH, UNITS + 3):
        stage1(t - 1) if t - 1 < UNITS else None
        stage0(t) if t < UNITS else None
        if NCH - 2 <= t - 2 < UNITS:
            stage2(t - 2)
        if t == NCH:
            stage3(NCH - 3)
        r = t - NCH
        if r < NCH:
            give_back(r)
        if r == NCH:
            each_peer(lambda k: route_copy(k).start())
            route_local().start()
        if NCH - 2 <= t - 3:
            stage3(t - 3)
        if r == 2:
            store(0, gd_ref, gd_hbm).start()
        if r >= 3 and r % 2 == 1 and (r - 3) // 2 < NCH:
            combine((r - 3) // 2)
        if t == UNITS:
            wait_bytes(got_r, rs_r.at[0])
            lane = lax.broadcasted_iota(jnp.int32, (EXP, CAP, 128), 2)
            slot = lax.broadcasted_iota(jnp.int32, (EXP, CAP, 128), 1)
            dots = jnp.sum(jnp.where(lane == slot, got_r[...], 0.0), axis=1)[:, :CAP]
            prob = prob_ref[0].astype(F32)
            live = live_mask()
            route_ref[0] = jnp.where(live, dots / jnp.where(live, prob, 1.0), 0.0).astype(BF)
            store(4, route_ref, route_hbm).start()
        if t == UNITS + 1:
            store(1, gg_ref, gg_hbm).start()
            store(3, tg_ref, tg_hbm).start()
    store(2, gu_ref, gu_hbm).start()
    for a in range(2):
        wait_bytes(weigh.at[pl.ds(0, 3)], info_s.at[a])
    for t in range(STEPS - SLOTS, STEPS):
        line_sent(t)
    for t in range(STEPS - SEND, STEPS):
        disp_sent(t)
    for c in range(NCH):
        wait_bytes(got_back.at[c, pl.ds(0, EXP - 1)], back_s.at[c])
    wait_bytes(got_r.at[pl.ds(0, EXP - 1)], rs_s.at[0])
    for u in range(UNITS - 2, UNITS):
        mate_copy(u).wait_send()
    for u in range(UNITS - 3, UNITS):
        ring_sent(u)
    for i, (src, dst) in enumerate((
            (gd_ref, gd_hbm), (gg_ref, gg_hbm), (gu_ref, gu_hbm), (tg_ref, tg_hbm), (route_ref, route_hbm))):
        store(i, src, dst).wait()


def finish(*refs):
    sources, results, held, sems = refs[:5], refs[5:10], refs[10:15], refs[15]
    loads = [pltpu.make_async_copy(a, b, sems.at[0, i]) for i, (a, b) in enumerate(zip(sources, held))]
    stores = [pltpu.make_async_copy(a, b, sems.at[1, i]) for i, (a, b) in enumerate(zip(held, results))]
    for copy in loads:
        copy.start()
    for i in (1, 2, 3, 4, 0):
        loads[i].wait()
        stores[i].start()
    for copy in stores:
        copy.wait()


def shards(tokens, out_grad, group_token, group_count, group_prob, w_gate, w_up, w_down):
    hbm = pl.BlockSpec(memory_space=pl.ANY)
    dma = pltpu.SemaphoreType.DMA
    results = pl.pallas_call(
        body,
        out_shape=(
            jax.ShapeDtypeStruct((TOK, D), BF),
            jax.ShapeDtypeStruct((1, EXP, CAP), BF),
            jax.ShapeDtypeStruct((D // 8, FF), BF),
            jax.ShapeDtypeStruct((D // 8, FF), BF),
            jax.ShapeDtypeStruct((FF, D // 8), BF),
        ),
        in_specs=[hbm] * 8,
        out_specs=[hbm] * 5,
        scratch_shapes=[
            pltpu.VMEM((1, EXP, CAP), jnp.int32), pltpu.VMEM((1, EXP), jnp.int32),
            pltpu.VMEM((1, EXP, CAP), BF), pltpu.VMEM((1, EXP, CAP), BF), dma((3,)),
            pltpu.VMEM((2, 2, LINE, LINE, CAP, TOK), BF),
            pltpu.VMEM((TOK, ROWS), BF),
            pltpu.VMEM((TOK, D), BF),
            pltpu.VMEM((D // 8, FF), BF), pltpu.VMEM((D // 8, FF), BF), pltpu.VMEM((FF, D // 8), BF),
            dma((5,)),
            pltpu.VMEM((LINE, LINE, CAP, TOK), BF),
            pltpu.VMEM((SLOTS, LINE, TOK, HALF), BF),
            pltpu.VMEM((SEND, LINE, LINE, CAP, HALF), BF),
            pltpu.VMEM((NCH, LINE, LINE, CAP, W), BF),
            pltpu.VMEM((NCH, LINE, LINE, CAP, W), BF),
            pltpu.VMEM((NWGU, W, 2 * FF), BF),
            pltpu.VMEM((NWD, FF, W), BF),
            pltpu.VMEM((ROWS, 2 * FF), F32),
            pltpu.VMEM((ROWS, FF), F32),
            pltpu.VMEM((ROWS, FF), BF),
            pltpu.VMEM((ROWS, 2 * FF), BF),
            pltpu.VMEM((NCH, EXP, CAP, W), BF),
            pltpu.VMEM((EXP, CAP, 128), F32),
            pltpu.VMEM((EXP, CAP, 128), F32),
            pltpu.VMEM((HALF, ROWS), BF),
            pltpu.VMEM((HALF, FF), F32),
            pltpu.VMEM((2, HALF, FF), BF),
            pltpu.VMEM((UNITS, HALF, FF), BF),
            pltpu.VMEM((3, 4, PIECE, FF), BF),
            pltpu.VMEM((UNITS, 2, PIECE // 2, FF), BF),
            pltpu.VMEM((UNITS, 2, PIECE // 2, FF), BF),
            pltpu.VMEM((UNITS, 2, PIECE // 2, FF), BF),
            dma((2,)), dma((2,)), dma((SLOTS,)), dma((SLOTS,)), dma((SLOTS, 3)),
            pltpu.SemaphoreType.REGULAR((SLOTS,)),
            dma((SEND,)), dma((STEPS,)),
            dma((NCH,)), dma((NCH,)),
            dma((1,)), dma((1,)),
            dma((NWGU,)), dma((NWD,)),
            dma((2,)), dma((UNITS,)), dma((3,)), dma((UNITS, 3)),
        ],
        compiler_params=pltpu.CompilerParams(
            collective_id=0, has_side_effects=True, vmem_limit_bytes=64 << 20),
        cost_estimate=pl.CostEstimate(flops=8 * 2 * ROWS * D * FF, bytes_accessed=40 << 20, transcendentals=ROWS * FF),
    )(group_token, group_count, group_prob, tokens, out_grad, w_gate[0], w_up[0], w_down[0])
    token_grad, route_grad, grad_gate, grad_up, grad_down = pl.pallas_call(
        finish,
        out_shape=tuple(jax.ShapeDtypeStruct(r.shape, r.dtype) for r in results),
        in_specs=[hbm] * 5,
        out_specs=[hbm] * 5,
        scratch_shapes=[pltpu.VMEM(r.shape, r.dtype) for r in results] + [dma((2, 5))],
        compiler_params=pltpu.CompilerParams(vmem_limit_bytes=60 << 20),
    )(*results)
    return token_grad, route_grad, grad_gate[None], grad_up[None], grad_down[None]


def solution(mesh):
    slots = P(("dp", "expert"), None, None)
    rows = P(("dp", "expert"), None)
    experts = P("expert", None, None)
    return jax.shard_map(
        shards, mesh=mesh,
        in_specs=(rows, rows, slots, rows, slots, experts, experts, experts),
        out_specs=(rows, slots, P("expert", "dp", None), P("expert", "dp", None), P("expert", None, "dp")),
        check_vma=False)
```

```python
import jax
import jax.numpy as jnp
from jax import lax
from jax.experimental import pallas as pl
from jax.experimental.pallas import tpu as pltpu
from jax.sharding import PartitionSpec as P

MESH = pl.DeviceIdType.MESH
BF = jnp.bfloat16
F32 = jnp.float32
D = 4096
FF = 768
TOK = 128
EXP = 16
CAP = 32
ROWS = EXP * CAP
NCH = 4
W = D // NCH
PIECE = W // 8
HALF = W // 2
UNITS = 3 * NCH
SEND = 4
LINE = 4
STEPS = 4 * NCH
SLOTS = 8
OPEN, PASS, PICK = 7, 5, 2
NWGU = 2
NWD = 2


def feature(chunk, block):
    return (2 * (block % 4) + block // 4) * (D // 8) + chunk * PIECE


def contract(left, right, dims):
    return lax.dot_general(left, right, (dims, ((), ())), preferred_element_type=F32)


def body(
    index_hbm, count_hbm, prob_hbm, tok_hbm, dy_hbm, wg_hbm, wu_hbm, wd_hbm,
    tg_hbm, route_hbm, gg_hbm, gu_hbm, gd_hbm,
    index_ref, count_ref, prob_ref, route_ref, in_sem, pick_ref, place_ref, tg_ref, gg_ref, gu_ref, gd_ref, out_sem, weigh, line, send, got_x, got_y, wgu, wdn, acc, hgrad, hidden, grads, got_back, rbuf, got_r,
    lhs_t, own, mate_out, mate_in, total, far, near, relay,
    info_s, info_r, fill_sem, line_s, line_r, free, disp_s, disp_r, back_s, back_r, rs_s, rs_r, wgu_sem, wdn_sem,
    mate_s, mate_r, ring_s, ring_r,
):
    dp = lax.axis_index("dp")
    me = lax.axis_index("expert")
    y, core = dp // 2, lax.rem(dp, 2)
    x, z = me // 4, lax.rem(me, 4)

    def peer(k):
        return lax.rem(x + k // 4, 4) * 4 + lax.rem(z + lax.rem(k, 4), 4)

    def on_expert(e):
        return {"dp": dp, "expert": e}

    mate = {"dp": y * 2 + 1 - core, "expert": me}
    y_dn, y_up, y_far = lax.rem(y + 3, 4), lax.rem(y + 1, 4), lax.rem(y + 2, 4)
    side = ({"dp": y_dn * 2 + core, "expert": me}, {"dp": y_up * 2 + core, "expert": me})

    def each_peer(fn):
        def step(i, carry):
            fn(1 + i)
            return carry
        lax.fori_loop(0, EXP - 1, step, 0)

    def wait_bytes(like, sem):
        pltpu.make_async_copy(like, like, sem).wait()

    def load_gu(chunk, slot):
        for b in range(8):
            rows = pl.ds(feature(chunk, b), PIECE)
            here = pl.ds(b * PIECE, PIECE)
            pltpu.make_async_copy(wg_hbm.at[rows, :], wgu.at[slot, here, pl.ds(0, FF)], wgu_sem.at[slot]).start()
            pltpu.make_async_copy(wu_hbm.at[rows, :], wgu.at[slot, here, pl.ds(FF, FF)], wgu_sem.at[slot]).start()

    def wait_gu(slot):
        pltpu.make_async_copy(wgu.at[slot], wgu.at[slot], wgu_sem.at[slot]).wait()

    def load_dn(chunk, slot):
        for b in range(8):
            pltpu.make_async_copy(
                wd_hbm.at[:, pl.ds(feature(chunk, b), PIECE)],
                wdn.at[slot, :, pl.ds(b * PIECE, PIECE)], wdn_sem.at[slot]).start()

    def wait_dn(slot):
        pltpu.make_async_copy(wdn.at[slot], wdn.at[slot], wdn_sem.at[slot]).wait()

    barrier = pltpu.get_barrier_semaphore()

    def greet(k):
        pl.semaphore_signal(barrier, inc=1, device_id=on_expert(peer(k)), device_id_type=MESH)

    for k in (1, 2, 3, 4, 8, 12):
        greet(k)
    for there in (mate, side[0], side[1]):
        pl.semaphore_signal(barrier, inc=1, device_id=there, device_id_type=MESH)

    def ends(t):
        return (x, lambda q: q * 4 + z) if t % 2 == 0 else (z, lambda q: x * 4 + q)

    def fill(t):
        source = tok_hbm if t < 2 * NCH else dy_hbm
        place = ends(t)[0]
        for b in range(4):
            pltpu.make_async_copy(
                source.at[:, pl.ds(feature((t // 2) % NCH, 4 * (t % 2) + b), PIECE)],
                line.at[t % SLOTS, place, :, pl.ds(b * PIECE, PIECE)], fill_sem.at[t % SLOTS]).start()

    def line_copy(t, i):
        place, expert_at = ends(t)
        up, dn = lax.rem(place + 1, LINE), lax.rem(place + 3, LINE)
        owner = (place, place, dn, up)[i]
        rows = (pl.ds(0, TOK), pl.ds(0, TOK), pl.ds(0, TOK // 2), pl.ds(TOK // 2, TOK // 2))[i]
        block = line.at[t % SLOTS, owner, rows, :]
        return pltpu.make_async_remote_copy(
            src_ref=block, dst_ref=block, send_sem=line_s.at[t % SLOTS], recv_sem=line_r.at[t % SLOTS, min(i, 2)],
            device_id=on_expert(expert_at((up, dn, up, dn)[i])), device_id_type=MESH)

    def line_sent(t):
        wait_bytes(line.at[t % SLOTS, pl.ds(0, 3)], line_s.at[t % SLOTS])

    def open_line(t):
        place = ends(t)[0]
        whole = line.at[t % SLOTS, place]
        pltpu.make_async_copy(whole, whole, fill_sem.at[t % SLOTS]).wait()
        if t >= SLOTS:
            pl.semaphore_wait(free.at[t - SLOTS], 2)
        line_copy(t, 0).start()
        line_copy(t, 1).start()

    def pass_line(t):
        line_copy(t, 0).wait_recv()
        line_copy(t, 2).start()
        line_copy(t, 1).wait_recv()
        line_copy(t, 3).start()

    def info_copy(a, d):
        place, expert_at = ends(a)
        there = lax.rem(place + d, LINE)
        return pltpu.make_async_remote_copy(
            src_ref=weigh.at[there] if a == 0 else weigh.at[:, there], dst_ref=pick_ref.at[a, 1, place],
            send_sem=info_s.at[a], recv_sem=info_r.at[a],
            device_id=on_expert(expert_at(there)), device_id_type=MESH)

    def column(values):
        owner = lax.broadcasted_iota(jnp.int32, (ROWS, EXP), 0) // CAP
        spread = (owner == lax.broadcasted_iota(jnp.int32, (ROWS, EXP), 1)).astype(BF)
        table = contract(spread, values.astype(BF), ((1,), (0,)))
        slot = lax.rem(lax.broadcasted_iota(jnp.int32, (ROWS, CAP), 0), CAP)
        return jnp.sum(jnp.where(slot == lax.broadcasted_iota(jnp.int32, (ROWS, CAP), 1), table, 0.0),
                       axis=1, keepdims=True)

    def live_mask():
        own = lax.broadcasted_iota(jnp.int32, (EXP, EXP), 0) == lax.broadcasted_iota(jnp.int32, (EXP, EXP), 1)
        count = jnp.sum(jnp.where(own, jnp.broadcast_to(count_ref[...].astype(F32), (EXP, EXP)), 0.0),
                        axis=1, keepdims=True)
        return lax.broadcasted_iota(jnp.int32, (EXP, CAP), 1).astype(F32) < count

    def describe():
        token = column(jnp.where(live_mask(), index_ref[0].astype(F32), -1.0))
        prob = column(prob_ref[0])
        hit = token == lax.broadcasted_iota(jnp.int32, (ROWS, TOK), 1).astype(F32)
        rows = jnp.where(hit, jnp.broadcast_to(prob, (ROWS, TOK)), 0.0).astype(BF)
        weigh[...] = rows.reshape(LINE, LINE, CAP, TOK)

    def select(a):
        wait_bytes(weigh.at[pl.ds(0, 3)], info_r.at[a])
        for q in range(LINE):
            pick_ref[a, 0, q] = jnp.where(pick_ref[a, 1, q].astype(F32) > 0.0, 1.0, 0.0).astype(BF)

    def selector():
        hit = weigh[...].reshape(ROWS, TOK).astype(F32) > 0.0
        place_ref[...] = jnp.where(hit, 1.0, 0.0).astype(BF).T

    def pick_rows(t):
        wait_bytes(line.at[t % SLOTS, 0], line_r.at[t % SLOTS, 2])
        if t >= SEND:
            disp_sent(t - SEND)
        kind = 0 if t < 2 * NCH else 1
        for q in range(LINE):
            rows = contract(pick_ref[t % 2, kind, q].reshape(LINE * CAP, TOK), line[t % SLOTS, q], ((1,), (0,)))
            send[t % SEND, :, q] = rows.astype(BF).reshape(LINE, CAP, HALF)
        disp_local(t).start()
        for d in range(1, LINE):
            disp_copy(t, d).start()
        if t + SLOTS < STEPS:
            place, expert_at = ends(t)
            line_sent(t)
            for q in (lax.rem(place + 1, LINE), lax.rem(place + 3, LINE)):
                pl.semaphore_signal(free.at[t], inc=1, device_id=on_expert(expert_at(q)), device_id_type=MESH)
            fill(t + SLOTS)

    def landing(t):
        buffer = (got_x if t < 2 * NCH else got_y).at[(t // 2) % NCH]
        cols = pl.ds((t % 2) * HALF, HALF)
        return buffer.at[:, z, :, cols] if t % 2 == 0 else buffer.at[x, :, :, cols]

    def disp_copy(t, d):
        place, expert_at = ends(t + 1)
        there = lax.rem(place + d, LINE)
        return pltpu.make_async_remote_copy(
            src_ref=send.at[t % SEND, there], dst_ref=landing(t),
            send_sem=disp_s.at[t % SEND], recv_sem=disp_r.at[t],
            device_id=on_expert(expert_at(there)), device_id_type=MESH)

    def disp_local(t):
        return pltpu.make_async_copy(send.at[t % SEND, ends(t + 1)[0]], landing(t), disp_r.at[t])

    def disp_sent(t):
        wait_bytes(send.at[t % SEND, pl.ds(0, 3)], disp_s.at[t % SEND])

    def disp_wait(t):
        buffer = (got_x if t < 2 * NCH else got_y).at[(t // 2) % NCH]
        wait_bytes(buffer.at[:, :, :, pl.ds((t % 2) * HALF, HALF)], disp_r.at[t])

    def unit(u):
        if u < NCH:
            return got_y.at[u], hidden, 0
        v = u - NCH
        return got_x.at[v // 2], grads, (v % 2) * FF

    def product(u, core_half, write):
        rows, right, col = unit(u)
        start = pl.multiple_of(core_half * HALF, HALF)
        lhs_t[...] = rows[:, :, :, pl.ds(start, HALF)].reshape(ROWS, HALF).T
        for n in range(3):
            cols = slice(n * 256, (n + 1) * 256)
            write(cols, contract(lhs_t[...], right[:, col + n * 256:col + (n + 1) * 256], ((1,), (0,))))

    def mate_copy(u):
        return pltpu.make_async_remote_copy(
            src_ref=mate_out.at[u % 2], dst_ref=mate_in.at[u], send_sem=mate_s.at[u % 2], recv_sem=mate_r.at[u],
            device_id=mate, device_id_type=MESH)

    def ring_copy(u, i):
        kind, way = i // 2, i % 2
        lower, upper = pl.ds(0, PIECE // 2), pl.ds(PIECE // 2, PIECE // 2)
        owner = (y_far, (y_dn, y_up)[way], (y_dn, y_up)[way])[kind]
        part = (lower, upper)[(way, 1 - way, way)[kind]]
        return pltpu.make_async_remote_copy(
            src_ref=total.at[u % 3, owner, part, :], dst_ref=(far, near, relay)[kind].at[u, way],
            send_sem=ring_s.at[u % 3], recv_sem=ring_r.at[u, min(i, 2)],
            device_id=side[way], device_id_type=MESH)

    def ring_sent(u):
        wait_bytes(total.at[u % 3, pl.ds(0, 3)], ring_s.at[u % 3])

    def stage0(u):
        if u >= 2:
            mate_copy(u - 2).wait_send()

        def to_mate(cols, value):
            mate_out[u % 2, :, cols] = value.astype(BF)

        def to_own(cols, value):
            own[:, cols] = value

        product(u, 1 - core, to_mate)
        mate_copy(u).start()
        product(u, core, to_own)

    def stage1(u):
        if u >= 3:
            ring_sent(u - 3)
        mate_copy(u).wait_recv()
        for q in range(4):
            rows = slice(q * PIECE, (q + 1) * PIECE)
            total[u % 3, q] = (own[rows, :] + mate_in[u, rows, :].astype(F32)).astype(BF)
        for i in range(4):
            ring_copy(u, i).start()

    def stage2(u):
        half = PIECE // 2
        for way, owner in ((0, y_dn), (1, y_up)):
            ring_copy(u, way).wait_recv()
            rows = slice(way * half, (way + 1) * half)
            total[u % 3, owner, rows, :] = (
                total[u % 3, owner, rows, :].astype(F32) + far[u, way].astype(F32)).astype(BF)
            ring_copy(u, 4 + way).start()

    def stage3(u):
        half = PIECE // 2
        wait_bytes(total.at[0, pl.ds(0, 2)], ring_r.at[u, 2])
        halves = []
        for h in range(2):
            rows = slice(h * half, (h + 1) * half)
            halves.append((total[u % 3, y, rows, :].astype(F32) + near[u, 1 - h].astype(F32)
                           + relay[u, h].astype(F32)) * 0.125)
        whole = jnp.concatenate(halves, axis=0)
        if u < NCH:
            gd_ref[:, u * PIECE:(u + 1) * PIECE] = whole.T.astype(BF)
        else:
            v = u - NCH
            (gg_ref, gu_ref)[v % 2][(v // 2) * PIECE:(v // 2 + 1) * PIECE, :] = whole.astype(BF)

    def tick(t):
        if 0 <= t - 1 < UNITS:
            stage1(t - 1)
        if t < UNITS:
            stage0(t)
        if 0 <= t - 2 < UNITS:
            stage2(t - 2)
        if 0 <= t - 3 < UNITS:
            stage3(t - 3)

    def forward(c):
        disp_wait(2 * c)
        disp_wait(2 * c + 1)
        wait_gu(c % NWGU)

        def step(n, carry):
            cols = pl.ds(pl.multiple_of(n * 256, 256), 256)
            part = contract(got_x[c].reshape(ROWS, W), wgu[c % NWGU, :, cols], ((1,), (0,)))
            if c == 0:
                acc[:, cols] = part
            else:
                acc[:, cols] += part
            return carry

        lax.fori_loop(0, 2 * FF // 256, step, 0)
        load_gu((c + NWGU) % NCH, c % NWGU)

    def activate():
        def step(i, carry):
            rows = pl.ds(pl.multiple_of(i * CAP, CAP), CAP)
            gate, up = acc[rows, :FF], acc[rows, FF:]
            sig = jax.nn.sigmoid(gate)
            act = gate * sig
            hidden[rows, :] = (act * up).astype(BF)
            acc[rows, :FF] = up * sig * (1.0 + gate * (1.0 - sig))
            acc[rows, FF:] = act
            return carry

        lax.fori_loop(0, EXP, step, 0)

    def landed(c):
        disp_wait(2 * (NCH + c))
        disp_wait(2 * (NCH + c) + 1)

    def backward(c):
        if c < NCH - 1:
            landed(c)
        wait_dn(c % NWD)
        rows = got_y[c].reshape(ROWS, W)
        for n in range(3):
            cols = slice(n * 256, (n + 1) * 256)
            part = contract(rows, wdn[c % NWD, cols, :], ((1,), (1,)))
            if c == 0:
                hgrad[:, cols] = part
            else:
                hgrad[:, cols] += part
        if c + NWD < NCH:
            load_dn(c + NWD, c % NWD)

    def route_copy(k):
        return pltpu.make_async_remote_copy(
            src_ref=rbuf.at[peer(k)], dst_ref=got_r.at[me], send_sem=rs_s.at[0], recv_sem=rs_r.at[0],
            device_id=on_expert(peer(k)), device_id_type=MESH)

    def route_local():
        return pltpu.make_async_copy(rbuf.at[me], got_r.at[me], rs_r.at[0])

    def differentiate():
        def step(i, carry):
            rows = pl.ds(pl.multiple_of(i * CAP, CAP), CAP)
            grad = hgrad[rows, :]
            grads[rows, :FF] = (grad * acc[rows, :FF]).astype(BF)
            grads[rows, FF:] = (grad * acc[rows, FF:]).astype(BF)
            dot = jnp.sum(grad * hidden[rows, :].astype(F32), axis=1, keepdims=True)
            rbuf[i] = jnp.broadcast_to(dot, (CAP, 128))
            return carry

        lax.fori_loop(0, EXP, step, 0)

    def back_copy(c, k):
        return pltpu.make_async_remote_copy(
            src_ref=got_y.at[c, lax.rem(x + k // 4, 4), lax.rem(z + lax.rem(k, 4), 4)], dst_ref=got_back.at[c, me], send_sem=back_s.at[c],
            recv_sem=back_r.at[c], device_id=on_expert(peer(k)), device_id_type=MESH)

    def back_local(c):
        return pltpu.make_async_copy(got_y.at[c, x, z], got_back.at[c, me], back_r.at[c])

    def give_back(c):
        wait_gu(c % NWGU)
        for n in range(W // 256):
            cols = slice(n * 256, (n + 1) * 256)
            part = contract(grads[...], wgu[c % NWGU, cols, :], ((1,), (1,)))
            got_y[c, :, :, :, cols] = part.astype(BF).reshape(LINE, LINE, CAP, 256)
        each_peer(lambda k: back_copy(c, k).start())
        back_local(c).start()
        if c + NWGU < NCH:
            load_gu(c + NWGU, c % NWGU)

    def combine(c):
        wait_bytes(got_back.at[c], back_r.at[c])
        for h in range(2):
            rows = got_back[c, :, :, h * HALF:(h + 1) * HALF].reshape(ROWS, HALF)
            part = contract(place_ref[...], rows, ((1,), (0,))).astype(BF)
            for b in range(4):
                f = feature(c, 4 * h + b)
                tg_ref[:, f:f + PIECE] = part[:, b * PIECE:(b + 1) * PIECE]

    def store(i, src, dst):
        return pltpu.make_async_copy(src, dst, out_sem.at[i])

    small = [pltpu.make_async_copy(a, b, in_sem.at[i]) for i, (a, b) in enumerate(
        ((index_hbm, index_ref), (count_hbm, count_ref), (prob_hbm, prob_ref)))]
    for copy in small:
        copy.start()
    for t in range(SLOTS):
        fill(t)
    for copy in small:
        copy.wait()
    describe()
    pick_ref[0, 1, x] = weigh[x]
    pick_ref[1, 1, z] = weigh[:, z]
    pl.semaphore_wait(barrier, 6 + 3)
    open_line(0)
    open_line(1)
    for a in range(2):
        for d in range(1, LINE):
            info_copy(a, d).start()
    for t in range(2, 4):
        open_line(t)
    pass_line(0)
    pass_line(1)
    select(0)
    open_line(4)
    pick_rows(0)
    select(1)
    open_line(5)
    pick_rows(1)
    load_gu(0, 0)
    pass_line(2)
    open_line(6)
    pass_line(3)
    load_gu(1, 1)
    pass_line(4)
    for c in range(NWD):
        load_dn(c, c)
    for t in range(STEPS):
        if t + PASS < STEPS:
            pass_line(t + PASS)
        if t + OPEN < STEPS:
            open_line(t + OPEN)
        if t + PICK < STEPS:
            pick_rows(t + PICK)
        c = t // 2
        if t % 2 == 1:
            if c < NCH:
                forward(c)
            else:
                if t == STEPS - 1:
                    landed(NCH - 1)
                    stage0(NCH - 1)
                backward(c - NCH)
        if t == 2:
            selector()
        if t == 2 * NCH - 1:
            activate()
        u = c - NCH
        if 0 <= u < NCH - 1 and t % 2 == 1:
            stage0(u)
            if u >= 2:
                stage3(u - 2)
        if 1 <= u and t % 2 == 0:
            stage1(u - 1)
            if u >= 2:
                stage2(u - 2)
    differentiate()
    for t in range(NCH, UNITS + 3):
        stage1(t - 1) if t - 1 < UNITS else None
        stage0(t) if t < UNITS else None
        if NCH - 2 <= t - 2 < UNITS:
            stage2(t - 2)
        if t == NCH:
            stage3(NCH - 3)
        r = t - NCH
        if r < NCH:
            give_back(r)
        if r == NCH:
            each_peer(lambda k: route_copy(k).start())
            route_local().start()
        if NCH - 2 <= t - 3:
            stage3(t - 3)
        if r == 2:
            store(0, gd_ref, gd_hbm).start()
        if r >= 3 and r % 2 == 1 and (r - 3) // 2 < NCH:
            combine((r - 3) // 2)
        if t == UNITS:
            wait_bytes(got_r, rs_r.at[0])
            lane = lax.broadcasted_iota(jnp.int32, (EXP, CAP, 128), 2)
            slot = lax.broadcasted_iota(jnp.int32, (EXP, CAP, 128), 1)
            dots = jnp.sum(jnp.where(lane == slot, got_r[...], 0.0), axis=1)[:, :CAP]
            prob = prob_ref[0].astype(F32)
            live = live_mask()
            route_ref[0] = jnp.where(live, dots / jnp.where(live, prob, 1.0), 0.0).astype(BF)
            store(4, route_ref, route_hbm).start()
        if t == UNITS + 1:
            store(1, gg_ref, gg_hbm).start()
            store(3, tg_ref, tg_hbm).start()
    store(2, gu_ref, gu_hbm).start()
    for a in range(2):
        wait_bytes(weigh.at[pl.ds(0, 3)], info_s.at[a])
    for t in range(STEPS - SLOTS, STEPS):
        line_sent(t)
    for t in range(STEPS - SEND, STEPS):
        disp_sent(t)
    for c in range(NCH):
        wait_bytes(got_back.at[c, pl.ds(0, EXP - 1)], back_s.at[c])
    wait_bytes(got_r.at[pl.ds(0, EXP - 1)], rs_s.at[0])
    for u in range(UNITS - 2, UNITS):
        mate_copy(u).wait_send()
    for u in range(UNITS - 3, UNITS):
        ring_sent(u)
    for i, (src, dst) in enumerate((
            (gd_ref, gd_hbm), (gg_ref, gg_hbm), (gu_ref, gu_hbm), (tg_ref, tg_hbm), (route_ref, route_hbm))):
        store(i, src, dst).wait()


def finish(*refs):
    sources, results, held, sems = refs[:5], refs[5:10], refs[10:15], refs[15]
    loads = [pltpu.make_async_copy(a, b, sems.at[0, i]) for i, (a, b) in enumerate(zip(sources, held))]
    stores = [pltpu.make_async_copy(a, b, sems.at[1, i]) for i, (a, b) in enumerate(zip(held, results))]
    for copy in loads:
        copy.start()
    for i in (1, 2, 3, 4, 0):
        loads[i].wait()
        stores[i].start()
    for copy in stores:
        copy.wait()


def shards(tokens, out_grad, group_token, group_count, group_prob, w_gate, w_up, w_down):
    hbm = pl.BlockSpec(memory_space=pl.ANY)
    dma = pltpu.SemaphoreType.DMA
    results = pl.pallas_call(
        body,
        out_shape=(
            jax.ShapeDtypeStruct((TOK, D), BF),
            jax.ShapeDtypeStruct((1, EXP, CAP), BF),
            jax.ShapeDtypeStruct((D // 8, FF), BF),
            jax.ShapeDtypeStruct((D // 8, FF), BF),
            jax.ShapeDtypeStruct((FF, D // 8), BF),
        ),
        in_specs=[hbm] * 8,
        out_specs=[hbm] * 5,
        scratch_shapes=[
            pltpu.VMEM((1, EXP, CAP), jnp.int32), pltpu.VMEM((1, EXP), jnp.int32),
            pltpu.VMEM((1, EXP, CAP), BF), pltpu.VMEM((1, EXP, CAP), BF), dma((3,)),
            pltpu.VMEM((2, 2, LINE, LINE, CAP, TOK), BF),
            pltpu.VMEM((TOK, ROWS), BF),
            pltpu.VMEM((TOK, D), BF),
            pltpu.VMEM((D // 8, FF), BF), pltpu.VMEM((D // 8, FF), BF), pltpu.VMEM((FF, D // 8), BF),
            dma((5,)),
            pltpu.VMEM((LINE, LINE, CAP, TOK), BF),
            pltpu.VMEM((SLOTS, LINE, TOK, HALF), BF),
            pltpu.VMEM((SEND, LINE, LINE, CAP, HALF), BF),
            pltpu.VMEM((NCH, LINE, LINE, CAP, W), BF),
            pltpu.VMEM((NCH, LINE, LINE, CAP, W), BF),
            pltpu.VMEM((NWGU, W, 2 * FF), BF),
            pltpu.VMEM((NWD, FF, W), BF),
            pltpu.VMEM((ROWS, 2 * FF), F32),
            pltpu.VMEM((ROWS, FF), F32),
            pltpu.VMEM((ROWS, FF), BF),
            pltpu.VMEM((ROWS, 2 * FF), BF),
            pltpu.VMEM((NCH, EXP, CAP, W), BF),
            pltpu.VMEM((EXP, CAP, 128), F32),
            pltpu.VMEM((EXP, CAP, 128), F32),
            pltpu.VMEM((HALF, ROWS), BF),
            pltpu.VMEM((HALF, FF), F32),
            pltpu.VMEM((2, HALF, FF), BF),
            pltpu.VMEM((UNITS, HALF, FF), BF),
            pltpu.VMEM((3, 4, PIECE, FF), BF),
            pltpu.VMEM((UNITS, 2, PIECE // 2, FF), BF),
            pltpu.VMEM((UNITS, 2, PIECE // 2, FF), BF),
            pltpu.VMEM((UNITS, 2, PIECE // 2, FF), BF),
            dma((2,)), dma((2,)), dma((SLOTS,)), dma((SLOTS,)), dma((SLOTS, 3)),
            pltpu.SemaphoreType.REGULAR((SLOTS,)),
            dma((SEND,)), dma((STEPS,)),
            dma((NCH,)), dma((NCH,)),
            dma((1,)), dma((1,)),
            dma((NWGU,)), dma((NWD,)),
            dma((2,)), dma((UNITS,)), dma((3,)), dma((UNITS, 3)),
        ],
        compiler_params=pltpu.CompilerParams(
            collective_id=0, has_side_effects=True, vmem_limit_bytes=64 << 20),
        cost_estimate=pl.CostEstimate(flops=8 * 2 * ROWS * D * FF, bytes_accessed=40 << 20, transcendentals=ROWS * FF),
    )(group_token, group_count, group_prob, tokens, out_grad, w_gate[0], w_up[0], w_down[0])
    token_grad, route_grad, grad_gate, grad_up, grad_down = pl.pallas_call(
        finish,
        out_shape=tuple(jax.ShapeDtypeStruct(r.shape, r.dtype) for r in results),
        in_specs=[hbm] * 5,
        out_specs=[hbm] * 5,
        scratch_shapes=[pltpu.VMEM(r.shape, r.dtype) for r in results] + [dma((2, 5))],
        compiler_params=pltpu.CompilerParams(vmem_limit_bytes=60 << 20),
    )(*results)
    return token_grad, route_grad, grad_gate[None], grad_up[None], grad_down[None]


def solution(mesh):
    slots = P(("dp", "expert"), None, None)
    rows = P(("dp", "expert"), None)
    experts = P("expert", None, None)
    return jax.shard_map(
        shards, mesh=mesh,
        in_specs=(rows, rows, slots, rows, slots, experts, experts, experts),
        out_specs=(rows, slots, P("expert", "dp", None), P("expert", "dp", None), P("expert", None, "dp")),
        check_vma=False)
```
